32 devices in a mesh: row: 4 (over y, x), col: 8 (over z, core).
Axes of the slice: x: 2, y: 2, z: 4, core: 2. Of those that a mesh axis runs over, the one named last changes fastest.
Arguments:
- image: bfloat16 [64, 128, 1280], P('row', 'col'), may hold values from -15 to 15
- stale_first: bfloat16 [64, 128, 1280], P('row', 'col'), may hold values from -6 to 6
- stale_normed: bfloat16 [64, 128, 1280], P('row', 'col'), may hold values from -5 to 5
- timestep: int32 [1], replicated, may hold values from 0 to 999
- time_weight: bfloat16 [320, 1280], replicated, may hold values from -0.3125 to 0.3125
- gain_first: float32 [1280], replicated, may hold values from 0.5 to 1.5
- shift_first: float32 [1280], replicated, may hold values from -3 to 3
- codes_first: int32 [9, 320, 1280], replicated, may hold values from 0 to 65535
- table_first: float32 [16, 1280], replicated, may hold values from -0.0546875 to 0.0546875
- bias_first: float32 [1280], replicated, may hold values from -3 to 3
- attn_gain: float32 [1280], replicated, may hold values from 0.5 to 1.5
- query_codes: int32 [320, 1280], replicated, may hold values from 0 to 65535
- query_table: float32 [16, 1280], replicated
- key_codes: int32 [320, 1280], replicated, may hold values from 0 to 65535
- key_table: float32 [16, 1280], replicated, may hold values from -0.15625 to 0.15625
- value_codes: int32 [320, 1280], replicated, may hold values from 0 to 65535
- value_table: float32 [16, 1280], replicated, may hold values from -0.15625 to 0.15625
- out_codes: int32 [320, 1280], replicated, may hold values from 0 to 65535
- out_table: float32 [16, 1280], replicated, may hold values from -0.15625 to 0.15625
Outputs:
- output: bfloat16 [64, 128, 1280], P('row', 'col')
The draws below stay inside these ranges and needn't reach their ends.
Inputs may be any that keep to these rules, and one draw needn't show every extreme that they name: `codes_first`: each word packs four 4-bit codes: the code of input channel 4 g + b lies in bits 4 b to 4 b + 3 of word g. `query_codes`: packed as codes_first. `key_codes`: packed as codes_first. `value_codes`: packed as codes_first. `out_codes`: packed as codes_first.
All inputs are finite; a program needn't handle non-finite values.
Results may differ from the reference program's by a relative error of at most 0.012.
Values may be sent and summed in bfloat16 or wider, within the bound.
No kernel may reach another device: no remote copies, remote signals or barrier semaphores. Data moves between devices by JAX's collectives and lax.ppermute only.
A program may use at most 192 MiB of HBM per device.

```python
import math
import jax
import jax.numpy as jnp
from jax import lax

C = 1280
HEADS = 20
HEAD_DIM = 64
GROUPS = 32
TEMB = 320
H_DEV = 16
W_DEV = 16
POOL = 4
NH = 64
NW = 128
N_ROW = 4
N_COL = 8


def draw_image(key, part):
    key = jax.random.fold_in(key, 3)
    row_scale = 0.5 + 1.5 * jnp.arange(NH, dtype=jnp.float32)[:, None, None] / NH
    col_scale = 1.0 + 0.5 * jnp.arange(NW, dtype=jnp.float32)[None, :, None] / NW
    noise = jax.random.truncated_normal(key, -5.0, 5.0, (NH, NW, C), jnp.float32)
    return (noise * row_scale * col_scale).astype(jnp.bfloat16)


def draw_stale_normed(key, part):
    key = jax.random.fold_in(key, 11)
    coarse_key, fine_key = jax.random.split(key)
    coarse_shape = (NH // POOL, 1, NW // POOL, 1, C)
    fine_shape = (NH // POOL, POOL, NW // POOL, POOL, C)
    coarse = jax.random.truncated_normal(coarse_key, -4.0, 4.0, coarse_shape, jnp.float32)
    fine = 0.2 * jax.random.truncated_normal(fine_key, -4.0, 4.0, fine_shape, jnp.float32)
    return (coarse + fine).reshape(NH, NW, C).astype(jnp.bfloat16)


def draw_query_table(key, part):
    key = jax.random.fold_in(key, 7)
    base = jax.random.uniform(key, (16, C), jnp.float32, -1.7, 1.7) * C ** (-0.5)
    return base * 3.0


def place_ends(entries, key, smallest, largest):
    shape = entries.shape
    place = [jax.random.randint(jax.random.fold_in(key, axis), (), 0, shape[axis]) for axis in range(len(shape))]
    entries = entries.at[tuple(place)].set(smallest)
    longest = shape.index(max(shape))
    place[longest] = (place[longest] + 1) % shape[longest]
    return entries.at[tuple(place)].set(largest)


def steps_of(key, extent, cuts, low, top_value):
    level = 1.0
    for position, shards_of in cuts:
        steps = jax.random.uniform(jax.random.fold_in(jax.random.fold_in(key, 6), position), (shards_of,), jnp.float32, low / len(cuts), top_value / len(cuts))
        level = level * jnp.repeat(jnp.exp(steps), extent[position] // shards_of).reshape((-1,) + (1,) * (len(extent) - 1 - position))
    return level


def scatter_about(own_key, shape, width, reach, cuts=(), kind=jnp.bfloat16):
    drawn = jax.random.normal(own_key, shape, jnp.float32) * width
    if len(cuts) > 0:
        drawn = steps_of(own_key, shape, cuts, -0.22, 0.18) * drawn
    return jnp.clip(drawn, min=-reach, max=reach).astype(kind)


def setup_inputs(seed: int = 0) -> dict:
    seeds = jax.random.split(jax.random.key(seed), 20)
    return {
        "image": draw_image(jax.random.fold_in(seeds[19], 71), 0),
        "stale_first": scatter_about(seeds[1], (NH, NW, C), 1.0, 6.0, ((0, 4), (1, 8))),
        "stale_normed": draw_stale_normed(jax.random.fold_in(seeds[19], 71), 0),
        "timestep": jax.random.randint(seeds[3], (1,), 0, 1000).astype(jnp.int32),
        "time_weight": scatter_about(seeds[4], (TEMB, C), TEMB ** -0.5, 0.3125),
        "gain_first": jnp.clip(1.0 + 0.1 * jax.random.normal(seeds[5], (C,), jnp.float32), 0.5, 1.5),
        "shift_first": scatter_about(seeds[6], (C,), 0.5, 3.0, (), jnp.float32),
        "codes_first": place_ends(jax.random.randint(seeds[7], (9, C // 4, C), 0, 65536), jax.random.fold_in(seeds[7], 1), 0, 65535).astype(jnp.int32),
        "table_first": scatter_about(seeds[8], (16, C), (9 * C) ** -0.5, 0.0546875, (), jnp.float32),
        "bias_first": scatter_about(seeds[9], (C,), 0.5, 3.0, (), jnp.float32),
        "attn_gain": jnp.clip(1.0 + 0.1 * jax.random.normal(seeds[10], (C,), jnp.float32), 0.5, 1.5),
        "query_codes": place_ends(jax.random.randint(seeds[11], (C // 4, C), 0, 65536), jax.random.fold_in(seeds[11], 1), 0, 65535).astype(jnp.int32),
        "query_table": draw_query_table(jax.random.fold_in(seeds[19], 71), 0),
        "key_codes": place_ends(jax.random.randint(seeds[13], (C // 4, C), 0, 65536), jax.random.fold_in(seeds[13], 1), 0, 65535).astype(jnp.int32),
        "key_table": scatter_about(seeds[14], (16, C), C ** -0.5, 0.15625, (), jnp.float32),
        "value_codes": place_ends(jax.random.randint(seeds[15], (C // 4, C), 0, 65536), jax.random.fold_in(seeds[15], 1), 0, 65535).astype(jnp.int32),
        "value_table": scatter_about(seeds[16], (16, C), C ** -0.5, 0.15625, (), jnp.float32),
        "out_codes": place_ends(jax.random.randint(seeds[17], (C // 4, C), 0, 65536), jax.random.fold_in(seeds[17], 1), 0, 65535).astype(jnp.int32),
        "out_table": scatter_about(seeds[18], (16, C), C ** -0.5, 0.15625, (), jnp.float32),
    }


def unpack_weight(packed, table):
    out_width = packed.shape[-1]
    shifts = 4 * jnp.arange(4, dtype=jnp.int32)
    nibbles = jnp.right_shift(packed[..., :, None, :], shifts[:, None]) & 15
    nibbles = nibbles.reshape(packed.shape[:-2] + (packed.shape[-2] * 4, out_width))
    levels = table.astype(jnp.bfloat16)
    weight = jnp.zeros(nibbles.shape, jnp.bfloat16)
    for code_value in range(16):
        weight = jnp.where(nibbles == code_value, levels[code_value], weight)
    return weight

def time_vector(timestep, time_weight):
    half_width = TEMB // 2
    frequency = jnp.exp(-math.log(10000.0) * jnp.arange(half_width, dtype=jnp.float32) / half_width)
    angles = timestep.astype(jnp.float32)[:, None] * frequency[None, :]
    sinusoid = jnp.concatenate([jnp.cos(angles), jnp.sin(angles)], axis=1).astype(jnp.bfloat16)
    return jax.nn.silu(jnp.dot(sinusoid, time_weight, preferred_element_type=jnp.float32))[0]

def norm_silu(values, gain, shift):
    grouped = values.reshape(-1, GROUPS, C // GROUPS)
    members = grouped.shape[0] * (C // GROUPS)
    average = lax.optimization_barrier(jnp.sum(grouped, axis=(0, 2))) / members
    mean_square = lax.optimization_barrier(jnp.sum(grouped * grouped, axis=(0, 2))) / members
    inv_std = lax.rsqrt(mean_square - average * average + 1e-05)
    normalized = ((grouped - average[None, :, None]) * inv_std[None, :, None]).reshape(values.shape)
    return jax.nn.silu(normalized * gain + shift).astype(jnp.bfloat16)

def stale_conv(current, stale, packed, table):
    padding = ((1, 1), (1, 1), (0, 0))
    current_pad = jnp.pad(current, padding)
    stale_pad = jnp.pad(stale, padding)
    row_index = jnp.arange(NH, dtype=jnp.int32)
    col_index = jnp.arange(NW, dtype=jnp.int32)
    summed = jnp.zeros((NH * NW, C), jnp.float32)
    for tap_index in range(9):
        row_step = tap_index // 3 - 1
        col_step = tap_index % 3 - 1
        same_row = (row_index + row_step) // H_DEV == row_index // H_DEV
        same_col = (col_index + col_step) // W_DEV == col_index // W_DEV
        inside = same_row[:, None, None] & same_col[None, :, None]
        source = jnp.where(inside, current_pad[1 + row_step:1 + row_step + NH, 1 + col_step:1 + col_step + NW], stale_pad[1 + row_step:1 + row_step + NH, 1 + col_step:1 + col_step + NW])
        summed = summed + jnp.dot(source.reshape(-1, C), unpack_weight(packed[tap_index], table), preferred_element_type=jnp.float32)
    return summed.reshape(NH, NW, C)

def layer_norm(values, gain):
    average = lax.optimization_barrier(jnp.mean(values, axis=-1, keepdims=True))
    centred = values - average
    spread = lax.optimization_barrier(jnp.mean(centred * centred, axis=-1, keepdims=True))
    return (centred * lax.rsqrt(spread + 1e-05) * gain).astype(jnp.bfloat16)

def attend(queries, key_rows, value_rows):
    count_rows = queries.shape[0]
    query_heads = queries.astype(jnp.float32).reshape(count_rows, HEADS, HEAD_DIM)
    key_heads = key_rows.astype(jnp.float32).reshape(-1, HEADS, HEAD_DIM)
    value_heads = value_rows.astype(jnp.float32).reshape(-1, HEADS, HEAD_DIM)
    scores = jnp.einsum('qhd,khd->hqk', query_heads, key_heads) / math.sqrt(HEAD_DIM)
    highest = lax.optimization_barrier(jnp.max(scores, axis=-1, keepdims=True))
    exponent = jnp.exp(scores - highest)
    weights = (exponent / lax.optimization_barrier(jnp.sum(exponent, axis=-1, keepdims=True))).astype(jnp.bfloat16)
    mixture = jnp.einsum('hqk,khd->qhd', weights.astype(jnp.float32), value_heads)
    return mixture.reshape(count_rows, C).astype(jnp.bfloat16)

def to_patches(values):
    return values.reshape(N_ROW, H_DEV, N_COL, W_DEV, C).transpose(0, 2, 1, 3, 4).reshape(N_ROW * N_COL, H_DEV * W_DEV, C)

def reference(image, stale_first, stale_normed, timestep, time_weight, gain_first, shift_first, codes_first, table_first, bias_first, attn_gain, query_codes, query_table, key_codes, key_table, value_codes, value_table, out_codes, out_table):
    time_shift = time_vector(timestep, time_weight)
    current = image.astype(jnp.float32)
    first_act = norm_silu(current, gain_first, shift_first)
    conv_one = stale_conv(first_act, stale_first, codes_first, table_first) + bias_first + time_shift
    residual = (current + conv_one).astype(jnp.bfloat16)
    normed = layer_norm(residual.astype(jnp.float32), attn_gain).reshape(-1, C)
    query_weight = unpack_weight(query_codes, query_table)
    key_weight = unpack_weight(key_codes, key_table)
    value_weight = unpack_weight(value_codes, value_table)
    out_weight = unpack_weight(out_codes, out_table)
    queries = jnp.dot(normed, query_weight, preferred_element_type=jnp.float32).astype(jnp.bfloat16)
    fresh_keys = jnp.dot(normed, key_weight, preferred_element_type=jnp.float32).astype(jnp.bfloat16)
    fresh_values = jnp.dot(normed, value_weight, preferred_element_type=jnp.float32).astype(jnp.bfloat16)
    pooled = stale_normed.astype(jnp.float32).reshape(NH // POOL, POOL, NW // POOL, POOL, C)
    pooled = lax.optimization_barrier(jnp.mean(pooled, axis=(1, 3))).reshape(-1, C).astype(jnp.bfloat16)
    stale_keys = jnp.dot(pooled, key_weight, preferred_element_type=jnp.float32).astype(jnp.bfloat16)
    stale_values = jnp.dot(pooled, value_weight, preferred_element_type=jnp.float32).astype(jnp.bfloat16)

    def one_patch(patch_block):
        patch_query, patch_keys, patch_values = patch_block
        return attend(patch_query, jnp.concatenate([patch_keys, stale_keys], axis=0), jnp.concatenate([patch_values, stale_values], axis=0))
    mixture = lax.map(one_patch, (to_patches(queries), to_patches(fresh_keys), to_patches(fresh_values)))
    mixture = mixture.reshape(N_ROW, N_COL, H_DEV, W_DEV, C).transpose(0, 2, 1, 3, 4).reshape(-1, C)
    output = residual.reshape(-1, C).astype(jnp.float32) + jnp.dot(mixture, out_weight, preferred_element_type=jnp.float32)
    return output.reshape(NH, NW, C).astype(jnp.bfloat16)
```

```python
import functools
import math

import jax
import jax.numpy as jnp
from jax import lax
from jax.experimental import pallas as pl
from jax.experimental.pallas import tpu as pltpu
from jax.sharding import PartitionSpec as P

HEAD_DIM = 64
GROUPS = 32
TEMB = 320
POOL = 4
LANES = 128
BF = jnp.bfloat16
F32 = jnp.float32
VMEM_LIMIT = 56 * 2**20


def params(**extra):
    return pltpu.CompilerParams(vmem_limit_bytes=VMEM_LIMIT, **extra)


def dot(a, b, **extra):
    return jnp.dot(a, b, preferred_element_type=F32, **extra)


def dot_t(a, b):
    return lax.dot_general(a, b, (((1,), (1,)), ((), ())), preferred_element_type=F32)


def iota(shape, dim):
    return lax.broadcasted_iota(jnp.int32, shape, dim)


def shuffle_matrix(words):
    size = 4 * words
    row = iota((size, size), 0)
    col = iota((size, size), 1)
    return (row == 4 * (col % words) + col // words).astype(F32).astype(BF)


def shuffle(values, words):
    size = 4 * words
    matrix = shuffle_matrix(words)
    return jnp.concatenate(
        [dot(values[:, k : k + size], matrix) for k in range(0, values.shape[1], size)], axis=1
    )


def group_matrix(channels, transposed):
    members = channels // GROUPS
    shape = (LANES, channels) if transposed else (channels, LANES)
    channel = iota(shape, 1 if transposed else 0)
    group = iota(shape, 0 if transposed else 1)
    return ((channel >= group * members) & (channel < (group + 1) * members)).astype(F32)


def first_kernel(core_ref, step_ref, image_ref, first_ref, normed_ref, time_ref, sums_ref, edge_ref, pool_ref, shift_ref):
    channels = image_ref.shape[-1]
    height, across = first_ref.shape[:2]
    cells = height * across
    core = core_ref[0]
    image = image_ref[...].reshape(cells, channels).astype(F32)
    sums = jnp.sum(image, axis=0, keepdims=True)
    squares = jnp.sum(image * image, axis=0, keepdims=True)
    row8 = iota((8, channels), 0)
    both = jnp.where(row8 == 0, sums, jnp.where(row8 == 1, squares, 0.0))
    sums_ref[...] = dot(both, group_matrix(channels, False), precision=lax.Precision.HIGHEST)

    cells_first = first_ref[...].reshape(cells, channels)
    row = iota((height, cells), 0)
    cell = iota((height, cells), 1)
    outer = jnp.where(core == 0, 0, across - 1)
    pick_outer = (cell == row * across + outer).astype(F32).astype(BF)
    pick_inner = (cell == row * across + (across - 1 - outer)).astype(F32).astype(BF)
    edge_ref[0] = dot(pick_outer, cells_first).astype(BF)
    edge_ref[1] = dot(pick_inner, cells_first).astype(BF)
    edge_ref[2] = first_ref[0]
    edge_ref[3] = first_ref[height - 1]

    pools = pool_ref.shape[0]
    pool = iota((pools, cells), 0)
    cell = iota((pools, cells), 1)
    in_row = cell // across // POOL == pool // (across // POOL)
    in_col = cell % across // POOL == pool % (across // POOL)
    average = jnp.where(in_row & in_col, 1.0 / (POOL * POOL), 0.0).astype(BF)
    pooled = dot(average, normed_ref[...].reshape(cells, channels)).astype(BF)
    pool_ref[...] = shuffle(pooled, 64).astype(BF)

    half = TEMB // 2
    place = iota((8, TEMB), 1)
    index = jnp.where(place < half, place, place - half).astype(F32)
    frequency = jnp.exp(-math.log(10000.0) * index / half)
    angle = step_ref[0].astype(F32) * frequency
    sinusoid = jnp.where(place < half, jnp.cos(angle), jnp.sin(angle)).astype(BF)
    shift = dot(sinusoid, time_ref[...])
    shift_ref[...] = shift * jax.nn.sigmoid(shift)


def first_pass(core, timestep, image, stale_first, stale_normed, time_weight):
    height, across, channels = image.shape
    pools = (height // POOL) * (across // POOL)
    whole = pl.BlockSpec(memory_space=pltpu.VMEM)
    small = pl.BlockSpec(memory_space=pltpu.SMEM)
    return pl.pallas_call(
        first_kernel,
        in_specs=[small, small] + [whole] * 4,
        out_specs=[whole] * 4,
        out_shape=[
            jax.ShapeDtypeStruct((8, LANES), F32),
            jax.ShapeDtypeStruct((4, height, channels), BF),
            jax.ShapeDtypeStruct((pools, channels), BF),
            jax.ShapeDtypeStruct((8, channels), F32),
        ],
        compiler_params=params(),
    )(core, timestep, image, stale_first, stale_normed, time_weight)


def decode_tile(words, words16, low, high, place):
    lows = []
    highs = []
    for k in range(0, words.shape[0], 8):
        index = words[k : k + 8]
        if place:
            index = index >> (4 * place)
        index = index & 7
        lows.append(jnp.take_along_axis(low, index, axis=0, mode="promise_in_bounds"))
        highs.append(jnp.take_along_axis(high, index, axis=0, mode="promise_in_bounds"))
    bit = 4 * place + 3
    upper = (words16 & jnp.int16(1 << bit if bit < 15 else -(1 << 15))) != 0
    return jnp.where(
        upper, jnp.concatenate(highs, axis=0).astype(BF), jnp.concatenate(lows, axis=0).astype(BF)
    )


def decode_kernel(core_ref, *refs, count, block):
    for k in range(count):
        codes_ref, table_ref, weight_ref = refs[2 * k], refs[2 * k + 1], refs[2 * count + k]
        decode_into(codes_ref, table_ref, weight_ref, block)


def decode_into(codes_ref, table_ref, weight_ref, block):
    words_all, columns = codes_ref.shape[-2:]
    lead = (0,) * (len(codes_ref.shape) - 2)
    for c in range(columns // LANES):
        lanes = pl.ds(c * LANES, LANES)
        low = table_ref[0:8, lanes]
        high = table_ref[8:16, lanes]
        for g in range(words_all // block):
            words = codes_ref[lead + (pl.ds(g * block, block), lanes)]
            words16 = words.astype(jnp.int16)
            for place in range(4):
                weight_ref[lead + (pl.ds((4 * g + place) * block, block), lanes)] = decode_tile(
                    words, words16, low, high, place
                )


def decode_cost(weights):
    return pl.CostEstimate(flops=8 * weights, bytes_accessed=3 * weights, transcendentals=0)


def decode_taps(core, codes, table, start, stop):
    words, channels = codes.shape[1:]
    half = channels // 2
    return pl.pallas_call(
        functools.partial(decode_kernel, count=1, block=64),
        grid_spec=pltpu.PrefetchScalarGridSpec(
            num_scalar_prefetch=1,
            grid=(stop - start,),
            in_specs=[
                pl.BlockSpec((1, words, half), lambda t, c: (start + t, 0, c[0])),
                pl.BlockSpec((16, half), lambda t, c: (0, c[0])),
            ],
            out_specs=[pl.BlockSpec((1, 4 * words, half), lambda t, c: (t, 0, 0))],
        ),
        out_shape=[jax.ShapeDtypeStruct((stop - start, 4 * words, half), BF)],
        compiler_params=params(),
        cost_estimate=decode_cost((stop - start) * 4 * words * half),
    )(core, codes, table)[0]


def decode_columns(core, *pairs):
    count = len(pairs) // 2
    words, channels = pairs[0].shape
    half = channels // 2
    return pl.pallas_call(
        functools.partial(decode_kernel, count=count, block=64),
        grid_spec=pltpu.PrefetchScalarGridSpec(
            num_scalar_prefetch=1,
            grid=(1,),
            in_specs=[
                pl.BlockSpec((words, half), lambda t, c: (0, c[0])),
                pl.BlockSpec((16, half), lambda t, c: (0, c[0])),
            ]
            * count,
            out_specs=[pl.BlockSpec((4 * words, half), lambda t, c: (0, 0))] * count,
        ),
        out_shape=[jax.ShapeDtypeStruct((4 * words, half), BF)] * count,
        compiler_params=params(),
        cost_estimate=decode_cost(count * 4 * words * half),
    )(core, *pairs)


def decode_rows(core, codes, table):
    words, channels = codes.shape
    half = words // 2
    return pl.pallas_call(
        functools.partial(decode_kernel, count=1, block=32),
        grid_spec=pltpu.PrefetchScalarGridSpec(
            num_scalar_prefetch=1,
            grid=(1,),
            in_specs=[
                pl.BlockSpec((half, channels), lambda t, c: (c[0], 0)),
                pl.BlockSpec((16, channels), lambda t, c: (0, 0)),
            ],
            out_specs=[pl.BlockSpec((4 * half, channels), lambda t, c: (0, 0))],
        ),
        out_shape=[jax.ShapeDtypeStruct((4 * half, channels), BF)],
        compiler_params=params(),
        cost_estimate=decode_cost(4 * half * channels),
    )(core, codes, table)[0]


def conv_kernel(
    core_ref, sums_ref, mine_ref, theirs_ref, rim_mine_ref, rim_theirs_ref, gain_ref, shift_ref, bias_ref, time_ref,
    half_mine_ref, half_theirs_ref, weight_ref, out_ref, act_ref, rim_ref, padded_ref, total_ref, *, members, split,
):
    tap = pl.program_id(0)
    taps = pl.num_programs(0)
    channels = gain_ref.shape[-1]
    height, across = mine_ref.shape[:2]
    cells = height * across
    core = core_ref[0]

    @pl.when(tap == 0)
    def _():
        spread = dot(sums_ref[...], group_matrix(channels, True), precision=lax.Precision.HIGHEST)
        average = spread[0:1] / members
        mean_square = spread[1:2] / members
        scale = lax.rsqrt(mean_square - average * average + 1e-05) * gain_ref[...]
        offset = shift_ref[...] - average * scale
        size = 256
        matrix = shuffle_matrix(64)
        for side, ref in enumerate((mine_ref, theirs_ref)):
            for k in range(0, channels, size):
                lanes = slice(k, k + size)
                value = ref[:, :, lanes].reshape(cells, size).astype(F32)
                value = value * scale[:, lanes] + offset[:, lanes]
                value = (0.5 * value) * (1.0 + jnp.tanh(0.5 * value))
                act_ref[side, :, lanes] = dot(value.astype(BF), matrix)
        for side, ref in enumerate((rim_mine_ref, rim_theirs_ref)):
            for k in range(0, channels, size):
                lanes = slice(k, k + size)
                rim_ref[side, :, lanes] = dot(ref[:, lanes], matrix)

        column = iota((across, channels), 0)

        def spread_row(side, line, value, left, right):
            padded_ref[side, 0, line] = jnp.where(column == 0, left, pltpu.roll(value, 1, 0)).astype(BF)
            padded_ref[side, 1, line] = value.astype(BF)
            padded_ref[side, 2, line] = jnp.where(
                column == across - 1, right, pltpu.roll(value, across - 1, 0)
            ).astype(BF)

        for side in range(2):
            other = 1 - side
            is_left = core == side
            for line, base in ((0, 0), (height + 1, 2 * across)):
                corner = across + (height - 1 if line == 0 else 0)
                far = rim_ref[side, base + corner : base + corner + 1]
                next_last = rim_ref[other, base + across - 1 : base + across]
                next_first = rim_ref[other, base : base + 1]
                value = rim_ref[side, base : base + across]
                spread_row(
                    side, line, value, jnp.where(is_left, far, next_last), jnp.where(is_left, next_first, far)
                )
            outer_at = 4 * across
            inner_at = 4 * across + height

            @pl.loop(0, height)
            def _(r):
                outer = rim_ref[side, pl.ds(outer_at + r, 1)]
                inner = rim_ref[other, pl.ds(inner_at + r, 1)]
                value = act_ref[side, pl.ds(pl.multiple_of(r * across, across), across)]
                spread_row(
                    side, r + 1, value, jnp.where(is_left, outer, inner), jnp.where(is_left, inner, outer)
                )

    row_start = tap // 3
    col_start = tap % 3
    source = padded_ref[:, col_start, pl.ds(row_start, height)].reshape(2 * cells, channels)
    part = dot(source, weight_ref[0])

    @pl.when(tap == 0)
    def _():
        total_ref[...] = part

    @pl.when((tap > 0) & (tap < taps - 1))
    def _():
        total_ref[...] += part

    @pl.when(tap == taps - 1)
    def _():
        extra = bias_ref[...] + time_ref[0:1]
        for side, ref in enumerate((half_mine_ref, half_theirs_ref)):
            image = ref[...].reshape(cells, -1).astype(F32)
            rows = slice(side * cells, (side + 1) * cells)
            conv = total_ref[rows] + part[rows] + extra
            out_ref[rows] = (image + conv).astype(BF)


def convolve(core, sums, mine, theirs, rim_mine, rim_theirs, gain, shift, bias, time_shift, weights, members):
    height, across, channels = mine.shape
    cells = height * across
    half = channels // 2
    whole = lambda *shape: pl.BlockSpec(shape, lambda t, c: (0,) * len(shape))
    part = lambda *shape: pl.BlockSpec(shape, lambda t, c: (0,) * (len(shape) - 1) + (c[0],))
    rim_rows = rim_mine.shape[0]
    return pl.pallas_call(
        functools.partial(conv_kernel, members=members, split=0),
        grid_spec=pltpu.PrefetchScalarGridSpec(
            num_scalar_prefetch=1,
            grid=(9,),
            in_specs=[
                whole(8, LANES),
                whole(height, across, channels),
                whole(height, across, channels),
                whole(rim_rows, channels),
                whole(rim_rows, channels),
                whole(1, channels),
                whole(1, channels),
                part(1, half),
                part(8, half),
                part(height, across, half),
                part(height, across, half),
                pl.BlockSpec((1, channels, half), lambda t, c: (t, 0, 0)),
            ],
            out_specs=whole(2 * cells, half),
            scratch_shapes=[
                pltpu.VMEM((2, cells, channels), F32),
                pltpu.VMEM((2, rim_rows, channels), F32),
                pltpu.VMEM((2, 3, height + 2, across, channels), BF),
                pltpu.VMEM((2 * cells, half), F32),
            ],
        ),
        out_shape=jax.ShapeDtypeStruct((2 * cells, half), BF),
        compiler_params=params(),
    )(core, sums, mine, theirs, rim_mine, rim_theirs, gain, shift, bias, time_shift, mine, theirs, weights)


def stale_kernel(near_ref, far_ref, key_ref, value_ref, keys_ref, values_ref):
    rows = near_ref.shape[0]
    for at, ref in ((0, near_ref), (rows, far_ref)):
        keys_ref[at : at + rows] = dot(ref[...], key_ref[...]).astype(BF)
        values_ref[at : at + rows] = dot(ref[...], value_ref[...]).astype(BF)


def stale_pass(near, far, key_weight, value_weight):
    rows, channels = near.shape
    half = key_weight.shape[1]
    whole = pl.BlockSpec(memory_space=pltpu.VMEM)
    return pl.pallas_call(
        stale_kernel,
        in_specs=[whole] * 4,
        out_specs=[whole] * 2,
        out_shape=[jax.ShapeDtypeStruct((2 * rows, half), BF)] * 2,
        compiler_params=params(),
        cost_estimate=pl.CostEstimate(
            flops=8 * rows * channels * half, bytes_accessed=4 * channels * half, transcendentals=0
        ),
    )(near, far, key_weight, value_weight)


def attention_kernel(
    core_ref, mine_ref, theirs_ref, gain_ref, query_ref, key_ref, value_ref, stale_keys_ref, stale_values_ref,
    out_weight_ref, partial_ref, rest_ref, normed_ref, q_ref, k_ref, v_ref, mixed_ref,
):
    rows, half = mine_ref.shape
    cells = rows // 2
    channels = 2 * half
    first = core_ref[0] == 0
    matrix = shuffle_matrix(64)
    for side in range(2):
        own = mine_ref[side * cells : (side + 1) * cells].astype(F32)
        other = theirs_ref[(1 - side) * cells : (2 - side) * cells].astype(F32)
        low = jnp.where(first, own, other)
        high = jnp.where(first, other, own)
        residual = jnp.concatenate([low, high], axis=1)
        if side == 0:
            rest_ref[...] = residual.astype(BF)
        average = jnp.sum(residual, axis=1, keepdims=True) / channels
        centred = residual - average
        deviation = jnp.sum(centred * centred, axis=1, keepdims=True) / channels
        normed = (centred * lax.rsqrt(deviation + 1e-05) * gain_ref[...]).astype(BF)
        for k in range(0, channels, 256):
            normed_ref[side * cells : (side + 1) * cells, k : k + 256] = dot(
                normed[:, k : k + 256], matrix
            ).astype(BF)
    normed = normed_ref[...]
    q_ref[...] = (dot(normed, query_ref[...]).astype(BF) * BF(1.0 / math.sqrt(HEAD_DIM))).astype(BF)
    k_ref[...] = dot(normed, key_ref[...]).astype(BF)
    v_ref[...] = dot(normed, value_ref[...]).astype(BF)

    ones = jnp.ones((cells, LANES), BF)
    stale_ones = jnp.ones((stale_keys_ref.shape[0], LANES), BF)
    lane = iota((cells, LANES), 1)
    for side in range(2):
        at = slice(side * cells, (side + 1) * cells)
        for pair in range(half // LANES):
            lanes = slice(pair * LANES, (pair + 1) * LANES)
            q = q_ref[at, lanes]
            zero = jnp.zeros_like(q)
            stacked = jnp.concatenate(
                [jnp.where(lane < HEAD_DIM, q, zero), jnp.where(lane < HEAD_DIM, zero, q)], axis=0
            )
            fresh = dot_t(stacked, k_ref[at, lanes])
            stale = dot_t(stacked, stale_keys_ref[:, lanes])
            highest = jnp.maximum(
                jnp.max(fresh, axis=1, keepdims=True), jnp.max(stale, axis=1, keepdims=True)
            )
            fresh = jnp.exp(fresh - highest).astype(BF)
            stale = jnp.exp(stale - highest).astype(BF)
            mixed = dot(fresh, jnp.concatenate([v_ref[at, lanes], ones], axis=1))
            mixed += dot(stale, jnp.concatenate([stale_values_ref[:, lanes], stale_ones], axis=1))
            mixed = mixed[:, :LANES] / mixed[:, LANES:]
            mixed_ref[at, lanes] = jnp.where(lane < HEAD_DIM, mixed[:cells], mixed[cells:]).astype(BF)
    mixture = shuffle(mixed_ref[...], 32).astype(BF)
    partial_ref[...] = dot(mixture, out_weight_ref[...]).astype(BF)


def attention_pass(core, mine, theirs, gain, query, key, value, stale_keys, stale_values, out_weight):
    rows, half = mine.shape
    channels = 2 * half
    cells = rows // 2
    whole = pl.BlockSpec(memory_space=pltpu.VMEM)
    small = pl.BlockSpec(memory_space=pltpu.SMEM)
    return pl.pallas_call(
        attention_kernel,
        in_specs=[small] + [whole] * 9,
        out_specs=[whole] * 2,
        out_shape=[
            jax.ShapeDtypeStruct((rows, channels), BF),
            jax.ShapeDtypeStruct((cells, channels), BF),
        ],
        scratch_shapes=[
            pltpu.VMEM((rows, channels), BF),
            pltpu.VMEM((rows, half), BF),
            pltpu.VMEM((rows, half), BF),
            pltpu.VMEM((rows, half), BF),
            pltpu.VMEM((rows, half), BF),
        ],
        compiler_params=params(),
    )(core, mine, theirs, gain, query, key, value, stale_keys, stale_values, out_weight)


def swap(values, axis, step):
    count = lax.axis_size(axis)
    return lax.ppermute(values, axis, [(i, i ^ step) for i in range(count)])


def total_over(values, axis):
    count = lax.axis_size(axis)
    if count & (count - 1):
        return lax.psum(values, axis)
    step = 1
    while step < count:
        values = values + swap(values, axis, step)
        step *= 2
    return values


def on_device(
    image,
    stale_first,
    stale_normed,
    timestep,
    time_weight,
    gain_first,
    shift_first,
    codes_first,
    table_first,
    bias_first,
    attn_gain,
    query_codes,
    query_table,
    key_codes,
    key_table,
    value_codes,
    value_table,
    out_codes,
    out_table,
):
    height, across, channels = image.shape
    cells = height * across
    rows = lax.axis_size("row")
    cols = lax.axis_size("col")
    members = cells * rows * cols * (channels // GROUPS)
    core = (lax.axis_index("col") % 2).astype(jnp.int32)[None]

    sums, edges, pooled, time_shift = first_pass(core, timestep, image, stale_first, stale_normed, time_weight)

    chips = [list(range(k, cols, 2)) for k in range(2)]
    near = lax.all_gather(pooled, "col", axis=0, tiled=True, axis_index_groups=chips)
    near = lax.all_gather(near, "row", axis=0, tiled=True)
    far = swap(near, "col", 1)

    partner_image = swap(image, "col", 1)
    between = [(i, i + 1) for i in range(1, cols - 1, 2)]
    outer = lax.ppermute(edges[0], "col", between + [(j, i) for i, j in between])
    above = lax.ppermute(
        jnp.concatenate([edges[3], outer]), "row", [(i, i + 1) for i in range(rows - 1)]
    )
    below = lax.ppermute(
        jnp.concatenate([edges[2], outer]), "row", [(i + 1, i) for i in range(rows - 1)]
    )
    rim = jnp.concatenate([above, below, outer, edges[1]])
    partner_rim = swap(rim, "col", 1)

    sums = total_over(total_over(sums, "col"), "row")

    weights = decode_taps(core, codes_first, table_first, 0, 9)
    query, key, value = decode_columns(
        core, query_codes, query_table, key_codes, key_table, value_codes, value_table
    )
    out_weight = decode_rows(core, out_codes, out_table)

    residual = convolve(
        core, sums, image, partner_image, rim, partner_rim, gain_first[None], shift_first[None],
        bias_first[None], time_shift, weights, members,
    )
    partner_residual = swap(residual, "col", 1)
    stale_keys, stale_values = stale_pass(near, far, key, value)
    partial, rest = attention_pass(
        core, residual, partner_residual, attn_gain[None], query, key, value, stale_keys, stale_values, out_weight
    )
    arrived = swap(partial[cells:], "col", 1)
    output = rest.astype(F32) + partial[:cells].astype(F32) + arrived.astype(F32)
    return output.astype(BF).reshape(height, across, channels)


def solution(mesh):
    split = P("row", "col", None)
    in_specs = (split,) * 3 + (P(),) * 16
    return jax.shard_map(on_device, mesh=mesh, in_specs=in_specs, out_specs=split, check_vma=False)
```

```python
import functools
import math

import jax
import jax.numpy as jnp
from jax import lax
from jax.experimental import pallas as pl
from jax.experimental.pallas import tpu as pltpu
from jax.sharding import PartitionSpec as P

HEAD_DIM = 64
GROUPS = 32
TEMB = 320
POOL = 4
LANES = 128
BF = jnp.bfloat16
F32 = jnp.float32


def params(mebibytes):
    return pltpu.CompilerParams(vmem_limit_bytes=mebibytes * 2**20)


def dot(a, b, **extra):
    return jnp.dot(a, b, preferred_element_type=F32, **extra)


def dot_t(a, b):
    return lax.dot_general(a, b, (((1,), (1,)), ((), ())), preferred_element_type=F32)


def iota(shape, dim):
    return lax.broadcasted_iota(jnp.int32, shape, dim)


def shuffle_matrix(words):
    size = 4 * words
    row = iota((size, size), 0)
    col = iota((size, size), 1)
    return (row == 4 * (col % words) + col // words).astype(F32).astype(BF)


def shuffle(values, words):
    size = 4 * words
    matrix = shuffle_matrix(words)
    return jnp.concatenate(
        [dot(values[:, k : k + size], matrix) for k in range(0, values.shape[1], size)], axis=1
    )


def group_matrix(channels, transposed):
    members = channels // GROUPS
    shape = (LANES, channels) if transposed else (channels, LANES)
    channel = iota(shape, 1 if transposed else 0)
    group = iota(shape, 0 if transposed else 1)
    return ((channel >= group * members) & (channel < (group + 1) * members)).astype(F32)


def first_kernel(core_ref, step_ref, image_ref, first_ref, normed_ref, time_ref, sums_ref, edge_ref, pool_ref, shift_ref):
    channels = image_ref.shape[-1]
    height, across = first_ref.shape[:2]
    cells = height * across
    core = core_ref[0]
    image = image_ref[...].reshape(cells, channels).astype(F32)
    sums = jnp.sum(image, axis=0, keepdims=True)
    squares = jnp.sum(image * image, axis=0, keepdims=True)
    row8 = iota((8, channels), 0)
    both = jnp.where(row8 == 0, sums, jnp.where(row8 == 1, squares, 0.0))
    sums_ref[...] = dot(both, group_matrix(channels, False), precision=lax.Precision.HIGHEST)

    cells_first = first_ref[...].reshape(cells, channels)
    row = iota((height, cells), 0)
    cell = iota((height, cells), 1)
    outer = jnp.where(core == 0, 0, across - 1)
    pick_outer = (cell == row * across + outer).astype(F32).astype(BF)
    pick_inner = (cell == row * across + (across - 1 - outer)).astype(F32).astype(BF)
    edge_ref[0] = dot(pick_outer, cells_first).astype(BF)
    edge_ref[1] = dot(pick_inner, cells_first).astype(BF)
    edge_ref[2] = first_ref[0]
    edge_ref[3] = first_ref[height - 1]

    pools = pool_ref.shape[0]
    pool = iota((pools, cells), 0)
    cell = iota((pools, cells), 1)
    in_row = cell // across // POOL == pool // (across // POOL)
    in_col = cell % across // POOL == pool % (across // POOL)
    average = jnp.where(in_row & in_col, 1.0 / (POOL * POOL), 0.0).astype(BF)
    pooled = dot(average, normed_ref[...].reshape(cells, channels)).astype(BF)
    pool_ref[...] = shuffle(pooled, 64).astype(BF)

    half = TEMB // 2
    place = iota((8, TEMB), 1)
    index = jnp.where(place < half, place, place - half).astype(F32)
    frequency = jnp.exp(-math.log(10000.0) * index / half)
    angle = step_ref[0].astype(F32) * frequency
    sinusoid = jnp.where(place < half, jnp.cos(angle), jnp.sin(angle)).astype(BF)
    shift = dot(sinusoid, time_ref[...])
    shift_ref[...] = shift * jax.nn.sigmoid(shift)


def first_pass(core, timestep, image, stale_first, stale_normed, time_weight):
    height, across, channels = image.shape
    pools = (height // POOL) * (across // POOL)
    whole = pl.BlockSpec(memory_space=pltpu.VMEM)
    small = pl.BlockSpec(memory_space=pltpu.SMEM)
    return pl.pallas_call(
        first_kernel,
        in_specs=[small, small] + [whole] * 4,
        out_specs=[whole] * 4,
        out_shape=[
            jax.ShapeDtypeStruct((8, LANES), F32),
            jax.ShapeDtypeStruct((4, height, channels), BF),
            jax.ShapeDtypeStruct((pools, channels), BF),
            jax.ShapeDtypeStruct((8, channels), F32),
        ],
        compiler_params=params(12),
    )(core, timestep, image, stale_first, stale_normed, time_weight)


def decode_tile(words, words16, low, high, place):
    lows = []
    highs = []
    for k in range(0, words.shape[0], 8):
        index = words[k : k + 8]
        if place:
            index = index >> (4 * place)
        index = index & 7
        lows.append(jnp.take_along_axis(low, index, axis=0, mode="promise_in_bounds"))
        highs.append(jnp.take_along_axis(high, index, axis=0, mode="promise_in_bounds"))
    bit = 4 * place + 3
    upper = (words16 & jnp.int16(1 << bit if bit < 15 else -(1 << 15))) != 0
    return jnp.where(
        upper, jnp.concatenate(highs, axis=0).astype(BF), jnp.concatenate(lows, axis=0).astype(BF)
    )


def decode_kernel(core_ref, *refs, count, block):
    for k in range(count):
        codes_ref, table_ref, weight_ref = refs[2 * k], refs[2 * k + 1], refs[2 * count + k]
        decode_into(codes_ref, table_ref, weight_ref, block)


def decode_into(codes_ref, table_ref, weight_ref, block):
    words_all, columns = codes_ref.shape[-2:]
    lead = (0,) * (len(codes_ref.shape) - 2)
    for c in range(columns // LANES):
        lanes = pl.ds(c * LANES, LANES)
        low = table_ref[0:8, lanes]
        high = table_ref[8:16, lanes]
        for g in range(words_all // block):
            words = codes_ref[lead + (pl.ds(g * block, block), lanes)]
            words16 = words.astype(jnp.int16)
            for place in range(4):
                weight_ref[lead + (pl.ds((4 * g + place) * block, block), lanes)] = decode_tile(
                    words, words16, low, high, place
                )


def decode_cost(weights):
    return pl.CostEstimate(flops=8 * weights, bytes_accessed=3 * weights, transcendentals=0)


def decode_taps(core, codes, table, weights, start, stop):
    words, channels = codes.shape[1:]
    half = channels // 2
    into = [] if weights is None else [weights]
    return pl.pallas_call(
        lambda core_ref, codes_ref, table_ref, *refs: decode_into(codes_ref, table_ref, refs[-1], 64),
        grid_spec=pltpu.PrefetchScalarGridSpec(
            num_scalar_prefetch=1,
            grid=(stop - start,),
            in_specs=[
                pl.BlockSpec((1, words, half), lambda t, c: (start + t, 0, c[0])),
                pl.BlockSpec((16, half), lambda t, c: (0, c[0])),
            ]
            + [pl.BlockSpec(memory_space=pl.ANY)] * len(into),
            out_specs=pl.BlockSpec((1, 4 * words, half), lambda t, c: (start + t, 0, 0)),
        ),
        out_shape=jax.ShapeDtypeStruct((codes.shape[0], 4 * words, half), BF),
        input_output_aliases={3: 0} if into else {},
        compiler_params=params(8),
        cost_estimate=decode_cost((stop - start) * 4 * words * half),
    )(core, codes, table, *into)


def decode_columns(core, *pairs):
    count = len(pairs) // 2
    words, channels = pairs[0].shape
    half = channels // 2
    return pl.pallas_call(
        functools.partial(decode_kernel, count=count, block=64),
        grid_spec=pltpu.PrefetchScalarGridSpec(
            num_scalar_prefetch=1,
            grid=(1,),
            in_specs=[
                pl.BlockSpec((words, half), lambda t, c: (0, c[0])),
                pl.BlockSpec((16, half), lambda t, c: (0, c[0])),
            ]
            * count,
            out_specs=[pl.BlockSpec((4 * words, half), lambda t, c: (0, 0))] * count,
        ),
        out_shape=[jax.ShapeDtypeStruct((4 * words, half), BF)] * count,
        compiler_params=params(14),
        cost_estimate=decode_cost(count * 4 * words * half),
    )(core, *pairs)


def decode_rows(core, codes, table):
    words, channels = codes.shape
    half = words // 2
    return pl.pallas_call(
        functools.partial(decode_kernel, count=1, block=32),
        grid_spec=pltpu.PrefetchScalarGridSpec(
            num_scalar_prefetch=1,
            grid=(1,),
            in_specs=[
                pl.BlockSpec((half, channels), lambda t, c: (c[0], 0)),
                pl.BlockSpec((16, channels), lambda t, c: (0, 0)),
            ],
            out_specs=[pl.BlockSpec((4 * half, channels), lambda t, c: (0, 0))],
        ),
        out_shape=[jax.ShapeDtypeStruct((4 * half, channels), BF)],
        compiler_params=params(10),
        cost_estimate=decode_cost(4 * half * channels),
    )(core, codes, table)[0]


def conv_kernel(
    core_ref, sums_ref, mine_ref, theirs_ref, rim_mine_ref, rim_theirs_ref, gain_ref, shift_ref, bias_ref, time_ref,
    weight_ref, out_ref, act_ref, rim_ref, padded_ref, total_ref, *, members,
):
    tap = pl.program_id(0)
    taps = pl.num_programs(0)
    channels = gain_ref.shape[-1]
    height, across = mine_ref.shape[:2]
    cells = height * across
    core = core_ref[0]

    @pl.when(tap == 0)
    def _():
        spread = dot(sums_ref[...], group_matrix(channels, True), precision=lax.Precision.HIGHEST)
        average = spread[0:1] / members
        mean_square = spread[1:2] / members
        scale = lax.rsqrt(mean_square - average * average + 1e-05) * gain_ref[...]
        offset = shift_ref[...] - average * scale
        size = 256
        matrix = shuffle_matrix(64)
        for side, ref in enumerate((mine_ref, theirs_ref)):
            for k in range(0, channels, size):
                lanes = slice(k, k + size)
                value = ref[:, :, lanes].reshape(cells, size).astype(F32)
                value = value * scale[:, lanes] + offset[:, lanes]
                value = (0.5 * value) * (1.0 + jnp.tanh(0.5 * value))
                act_ref[side, :, lanes] = dot(value.astype(BF), matrix)
        for side, ref in enumerate((rim_mine_ref, rim_theirs_ref)):
            for k in range(0, channels, size):
                lanes = slice(k, k + size)
                rim_ref[side, :, lanes] = dot(ref[:, lanes], matrix)

        column = iota((across, channels), 0)

        def spread_row(side, line, value, left, right):
            padded_ref[side, 0, line] = jnp.where(column == 0, left, pltpu.roll(value, 1, 0)).astype(BF)
            padded_ref[side, 1, line] = value.astype(BF)
            padded_ref[side, 2, line] = jnp.where(
                column == across - 1, right, pltpu.roll(value, across - 1, 0)
            ).astype(BF)

        for side in range(2):
            other = 1 - side
            is_left = core == side
            for line, base in ((0, 0), (height + 1, 2 * across)):
                corner = across + (height - 1 if line == 0 else 0)
                far = rim_ref[side, base + corner : base + corner + 1]
                next_last = rim_ref[other, base + across - 1 : base + across]
                next_first = rim_ref[other, base : base + 1]
                value = rim_ref[side, base : base + across]
                spread_row(
                    side, line, value, jnp.where(is_left, far, next_last), jnp.where(is_left, next_first, far)
                )
            outer_at = 4 * across
            inner_at = 4 * across + height

            @pl.loop(0, height)
            def _(r):
                outer = rim_ref[side, pl.ds(outer_at + r, 1)]
                inner = rim_ref[other, pl.ds(inner_at + r, 1)]
                value = act_ref[side, pl.ds(pl.multiple_of(r * across, across), across)]
                spread_row(
                    side, r + 1, value, jnp.where(is_left, outer, inner), jnp.where(is_left, inner, outer)
                )

    row_start = tap // 3
    col_start = tap % 3
    source = padded_ref[:, col_start, pl.ds(row_start, height)].reshape(2 * cells, channels)
    part = dot(source, weight_ref[0])

    @pl.when(tap == 0)
    def _():
        total_ref[...] = part

    @pl.when((tap > 0) & (tap < taps - 1))
    def _():
        total_ref[...] += part

    @pl.when(tap == taps - 1)
    def _():
        extra = bias_ref[...] + time_ref[0:1]
        half = channels // 2
        for side, ref in enumerate((mine_ref, theirs_ref)):
            image = jnp.where(core == 0, ref[:, :, :half], ref[:, :, half:]).reshape(cells, half).astype(F32)
            rows = slice(side * cells, (side + 1) * cells)
            conv = total_ref[rows] + part[rows] + extra
            out_ref[rows] = (image + conv).astype(BF)


def convolve(core, sums, mine, theirs, rim_mine, rim_theirs, gain, shift, bias, time_shift, weights, members):
    height, across, channels = mine.shape
    cells = height * across
    half = channels // 2
    whole = lambda *shape: pl.BlockSpec(shape, lambda t, c: (0,) * len(shape))
    part = lambda *shape: pl.BlockSpec(shape, lambda t, c: (0,) * (len(shape) - 1) + (c[0],))
    rim_rows = rim_mine.shape[0]
    return pl.pallas_call(
        functools.partial(conv_kernel, members=members),
        grid_spec=pltpu.PrefetchScalarGridSpec(
            num_scalar_prefetch=1,
            grid=(9,),
            in_specs=[
                whole(8, LANES),
                whole(height, across, channels),
                whole(height, across, channels),
                whole(rim_rows, channels),
                whole(rim_rows, channels),
                whole(1, channels),
                whole(1, channels),
                part(1, half),
                part(8, half),
                pl.BlockSpec((1, channels, half), lambda t, c: (t, 0, 0)),
            ],
            out_specs=whole(2 * cells, half),
            scratch_shapes=[
                pltpu.VMEM((2, cells, channels), F32),
                pltpu.VMEM((2, rim_rows, channels), F32),
                pltpu.VMEM((2, 3, height + 2, across, channels), BF),
                pltpu.VMEM((2 * cells, half), F32),
            ],
        ),
        out_shape=jax.ShapeDtypeStruct((2 * cells, half), BF),
        compiler_params=params(24),
    )(core, sums, mine, theirs, rim_mine, rim_theirs, gain, shift, bias, time_shift, weights)


def stale_kernel(near_ref, far_ref, key_ref, value_ref, keys_ref, values_ref):
    rows = near_ref.shape[0]
    for at, ref in ((0, near_ref), (rows, far_ref)):
        keys_ref[at : at + rows] = dot(ref[...], key_ref[...]).astype(BF)
        values_ref[at : at + rows] = dot(ref[...], value_ref[...]).astype(BF)


def stale_pass(near, far, key_weight, value_weight):
    rows, channels = near.shape
    half = key_weight.shape[1]
    whole = pl.BlockSpec(memory_space=pltpu.VMEM)
    return pl.pallas_call(
        stale_kernel,
        in_specs=[whole] * 4,
        out_specs=[whole] * 2,
        out_shape=[jax.ShapeDtypeStruct((2 * rows, half), BF)] * 2,
        compiler_params=params(20),
        cost_estimate=pl.CostEstimate(
            flops=8 * rows * channels * half, bytes_accessed=4 * channels * half, transcendentals=0
        ),
    )(near, far, key_weight, value_weight)


def attention_kernel(
    core_ref, mine_ref, theirs_ref, gain_ref, query_ref, key_ref, value_ref, stale_keys_ref, stale_values_ref,
    out_weight_ref, send_ref, keep_ref, normed_ref, q_ref, k_ref, v_ref, mixed_ref,
):
    rows, half = mine_ref.shape
    cells = rows // 2
    channels = 2 * half
    first = core_ref[0] == 0
    matrix = shuffle_matrix(64)
    for side in range(2):
        own = mine_ref[side * cells : (side + 1) * cells].astype(F32)
        other = theirs_ref[(1 - side) * cells : (2 - side) * cells].astype(F32)
        low = jnp.where(first, own, other)
        high = jnp.where(first, other, own)
        residual = jnp.concatenate([low, high], axis=1)
        if side == 0:
            keep_ref[...] = residual
        average = jnp.sum(residual, axis=1, keepdims=True) / channels
        centred = residual - average
        deviation = jnp.sum(centred * centred, axis=1, keepdims=True) / channels
        normed = (centred * lax.rsqrt(deviation + 1e-05) * gain_ref[...]).astype(BF)
        for k in range(0, channels, 256):
            normed_ref[side * cells : (side + 1) * cells, k : k + 256] = dot(
                normed[:, k : k + 256], matrix
            ).astype(BF)
    normed = normed_ref[...]
    q_ref[...] = (dot(normed, query_ref[...]).astype(BF) * BF(1.0 / math.sqrt(HEAD_DIM))).astype(BF)
    k_ref[...] = dot(normed, key_ref[...]).astype(BF)
    v_ref[...] = dot(normed, value_ref[...]).astype(BF)

    ones = jnp.ones((cells, LANES), BF)
    stale_ones = jnp.ones((stale_keys_ref.shape[0], LANES), BF)
    lane = iota((cells, LANES), 1)
    for side in range(2):
        at = slice(side * cells, (side + 1) * cells)
        for pair in range(half // LANES):
            lanes = slice(pair * LANES, (pair + 1) * LANES)
            q = q_ref[at, lanes]
            zero = jnp.zeros_like(q)
            stacked = jnp.concatenate(
                [jnp.where(lane < HEAD_DIM, q, zero), jnp.where(lane < HEAD_DIM, zero, q)], axis=0
            )
            fresh = dot_t(stacked, k_ref[at, lanes])
            stale = dot_t(stacked, stale_keys_ref[:, lanes])
            highest = jnp.maximum(
                jnp.max(fresh, axis=1, keepdims=True), jnp.max(stale, axis=1, keepdims=True)
            )
            fresh = jnp.exp(fresh - highest).astype(BF)
            stale = jnp.exp(stale - highest).astype(BF)
            mixed = dot(fresh, jnp.concatenate([v_ref[at, lanes], ones], axis=1))
            mixed += dot(stale, jnp.concatenate([stale_values_ref[:, lanes], stale_ones], axis=1))
            mixed = mixed[:, :LANES] / mixed[:, LANES:]
            mixed_ref[at, lanes] = jnp.where(lane < HEAD_DIM, mixed[:cells], mixed[cells:]).astype(BF)
    mixture = shuffle(mixed_ref[...], 32).astype(BF)
    send_ref[...] = dot(mixture[cells:], out_weight_ref[...]).astype(BF)
    keep_ref[...] += dot(mixture[:cells], out_weight_ref[...])


def attention_pass(core, mine, theirs, gain, query, key, value, stale_keys, stale_values, out_weight):
    rows, half = mine.shape
    channels = 2 * half
    cells = rows // 2
    whole = pl.BlockSpec(memory_space=pltpu.VMEM)
    small = pl.BlockSpec(memory_space=pltpu.SMEM)
    return pl.pallas_call(
        attention_kernel,
        in_specs=[small] + [whole] * 9,
        out_specs=[whole] * 2,
        out_shape=[
            jax.ShapeDtypeStruct((cells, channels), BF),
            jax.ShapeDtypeStruct((cells, channels), F32),
        ],
        scratch_shapes=[
            pltpu.VMEM((rows, channels), BF),
            pltpu.VMEM((rows, half), BF),
            pltpu.VMEM((rows, half), BF),
            pltpu.VMEM((rows, half), BF),
            pltpu.VMEM((rows, half), BF),
        ],
        compiler_params=params(28),
    )(core, mine, theirs, gain, query, key, value, stale_keys, stale_values, out_weight)


def swap(values, axis, step):
    count = lax.axis_size(axis)
    return lax.ppermute(values, axis, [(i, i ^ step) for i in range(count)])


def steps_over(axis, first):
    count = lax.axis_size(axis)
    steps = []
    while first < count:
        steps.append((axis, first))
        first *= 2
    return steps


def tie(first, second):
    return lax.optimization_barrier((first, second))


def on_device(
    image,
    stale_first,
    stale_normed,
    timestep,
    time_weight,
    gain_first,
    shift_first,
    codes_first,
    table_first,
    bias_first,
    attn_gain,
    query_codes,
    query_table,
    key_codes,
    key_table,
    value_codes,
    value_table,
    out_codes,
    out_table,
):
    height, across, channels = image.shape
    cells = height * across
    rows = lax.axis_size("row")
    cols = lax.axis_size("col")
    members = cells * rows * cols * (channels // GROUPS)
    core = (lax.axis_index("col") % 2).astype(jnp.int32)[None]

    sums, edges, pooled, time_shift = first_pass(core, timestep, image, stale_first, stale_normed, time_weight)

    between = [(i, i + 1) for i in range(1, cols - 1, 2)]
    sum_steps = steps_over("col", 1) + steps_over("row", 1)
    pool_steps = steps_over("col", 2) + steps_over("row", 1)
    chunks = [(0, 2), (2, 4), (4, 6), (6, 9)]
    slots = max(len(sum_steps), len(pool_steps), len(chunks))
    weights = None
    near = pooled
    codes = codes_first
    for slot in range(slots):
        if weights is not None:
            (sums, near), weights = tie((sums, near), weights)
        if slot == 0:
            outer = lax.ppermute(edges[0], "col", between + [(j, i) for i, j in between])
        elif slot == 1:
            above = lax.ppermute(
                jnp.concatenate([edges[3], outer]), "row", [(i, i + 1) for i in range(rows - 1)]
            )
            below = lax.ppermute(
                jnp.concatenate([edges[2], outer]), "row", [(i + 1, i) for i in range(rows - 1)]
            )
        elif slot == 2:
            rim = jnp.concatenate([above, below, outer, edges[1]])
            partner_rim = swap(rim, "col", 1)
        elif slot == 3:
            partner_image = swap(image, "col", 1)
        next_sums = sums + swap(sums, *sum_steps[slot]) if slot < len(sum_steps) else sums
        next_near = jnp.concatenate([near, swap(near, *pool_steps[slot])]) if slot < len(pool_steps) else near
        if slot < len(chunks):
            _, codes = tie((sums, near), codes)
            weights = decode_taps(core, codes, table_first, weights, *chunks[slot])
        sums = next_sums
        near = next_near
    far = swap(near, "col", 1)
    query, key, value = decode_columns(
        core, query_codes, query_table, key_codes, key_table, value_codes, value_table
    )
    residual = convolve(
        core, sums, image, partner_image, rim, partner_rim, gain_first[None], shift_first[None],
        bias_first[None], time_shift, weights, members,
    )
    partner_residual = swap(residual, "col", 1)
    (residual, out_codes), _ = tie((residual, out_codes), residual)
    out_weight = decode_rows(core, out_codes, out_table)
    stale_keys, stale_values = stale_pass(near, far, key, value)
    send, keep = attention_pass(
        core, residual, partner_residual, attn_gain[None], query, key, value, stale_keys, stale_values, out_weight
    )
    output = keep + swap(send, "col", 1).astype(F32)
    return output.astype(BF).reshape(height, across, channels)


def solution(mesh):
    split = P("row", "col", None)
    in_specs = (split,) * 3 + (P(),) * 16
    return jax.shard_map(on_device, mesh=mesh, in_specs=in_specs, out_specs=split, check_vma=False)
```

```python
import functools
import math

import jax
import jax.numpy as jnp
from jax import lax
from jax.experimental import pallas as pl
from jax.experimental.pallas import tpu as pltpu
from jax.sharding import PartitionSpec as P

HEAD_DIM = 64
GROUPS = 32
TEMB = 320
POOL = 4
LANES = 128
BF = jnp.bfloat16
F32 = jnp.float32


def params(mebibytes):
    return pltpu.CompilerParams(vmem_limit_bytes=mebibytes * 2**20)


def dot(a, b, **extra):
    return jnp.dot(a, b, preferred_element_type=F32, **extra)


def dot_t(a, b):
    return lax.dot_general(a, b, (((1,), (1,)), ((), ())), preferred_element_type=F32)


def iota(shape, dim):
    return lax.broadcasted_iota(jnp.int32, shape, dim)


def shuffle_matrix(words):
    size = 4 * words
    row = iota((size, size), 0)
    col = iota((size, size), 1)
    return (row == 4 * (col % words) + col // words).astype(F32).astype(BF)


def shuffle(values, words):
    size = 4 * words
    matrix = shuffle_matrix(words)
    return jnp.concatenate(
        [dot(values[:, k : k + size], matrix) for k in range(0, values.shape[1], size)], axis=1
    )


def group_matrix(channels, transposed):
    members = channels // GROUPS
    shape = (LANES, channels) if transposed else (channels, LANES)
    channel = iota(shape, 1 if transposed else 0)
    group = iota(shape, 0 if transposed else 1)
    return ((channel >= group * members) & (channel < (group + 1) * members)).astype(F32)


def first_kernel(core_ref, step_ref, image_ref, first_ref, normed_ref, time_ref, sums_ref, edge_ref, pool_ref, shift_ref):
    channels = image_ref.shape[-1]
    height, across = first_ref.shape[:2]
    cells = height * across
    core = core_ref[0]
    image = image_ref[...].reshape(cells, channels).astype(F32)
    sums = jnp.sum(image, axis=0, keepdims=True)
    squares = jnp.sum(image * image, axis=0, keepdims=True)
    row8 = iota((8, channels), 0)
    both = jnp.where(row8 == 0, sums, jnp.where(row8 == 1, squares, 0.0))
    sums_ref[...] = dot(both, group_matrix(channels, False), precision=lax.Precision.HIGHEST)[0:2]

    cells_first = first_ref[...].reshape(cells, channels)
    row = iota((height, cells), 0)
    cell = iota((height, cells), 1)
    outer = jnp.where(core == 0, 0, across - 1)
    pick_outer = (cell == row * across + outer).astype(F32).astype(BF)
    pick_inner = (cell == row * across + (across - 1 - outer)).astype(F32).astype(BF)
    edge_ref[0] = dot(pick_outer, cells_first).astype(BF)
    edge_ref[1] = dot(pick_inner, cells_first).astype(BF)
    edge_ref[2] = first_ref[0]
    edge_ref[3] = first_ref[height - 1]

    pools = pool_ref.shape[0]
    pool = iota((pools, cells), 0)
    cell = iota((pools, cells), 1)
    in_row = cell // across // POOL == pool // (across // POOL)
    in_col = cell % across // POOL == pool % (across // POOL)
    average = jnp.where(in_row & in_col, 1.0 / (POOL * POOL), 0.0).astype(BF)
    pooled = dot(average, normed_ref[...].reshape(cells, channels)).astype(BF)
    pool_ref[...] = shuffle(pooled, 64).astype(BF)

    half = TEMB // 2
    place = iota((8, TEMB), 1)
    index = jnp.where(place < half, place, place - half).astype(F32)
    frequency = jnp.exp(-math.log(10000.0) * index / half)
    angle = step_ref[0].astype(F32) * frequency
    sinusoid = jnp.where(place < half, jnp.cos(angle), jnp.sin(angle)).astype(BF)
    shift = dot(sinusoid, time_ref[...])
    shift_ref[...] = shift * jax.nn.sigmoid(shift)


def first_pass(core, timestep, image, stale_first, stale_normed, time_weight):
    height, across, channels = image.shape
    pools = (height // POOL) * (across // POOL)
    whole = pl.BlockSpec(memory_space=pltpu.VMEM)
    small = pl.BlockSpec(memory_space=pltpu.SMEM)
    return pl.pallas_call(
        first_kernel,
        in_specs=[small, small] + [whole] * 4,
        out_specs=[whole] * 4,
        out_shape=[
            jax.ShapeDtypeStruct((2, LANES), F32),
            jax.ShapeDtypeStruct((4, height, channels), BF),
            jax.ShapeDtypeStruct((pools, channels), BF),
            jax.ShapeDtypeStruct((8, channels), F32),
        ],
        compiler_params=params(12),
    )(core, timestep, image, stale_first, stale_normed, time_weight)


def decode_tile(words, words16, low, high, place):
    lows = []
    highs = []
    for k in range(0, words.shape[0], 8):
        index = words[k : k + 8]
        if place:
            index = index >> (4 * place)
        index = index & 7
        lows.append(jnp.take_along_axis(low, index, axis=0, mode="promise_in_bounds"))
        highs.append(jnp.take_along_axis(high, index, axis=0, mode="promise_in_bounds"))
    bit = 4 * place + 3
    upper = (words16 & jnp.int16(1 << bit if bit < 15 else -(1 << 15))) != 0
    return jnp.where(
        upper, jnp.concatenate(highs, axis=0).astype(BF), jnp.concatenate(lows, axis=0).astype(BF)
    )


def decode_kernel(core_ref, *refs, count, block):
    for k in range(count):
        codes_ref, table_ref, weight_ref = refs[2 * k], refs[2 * k + 1], refs[2 * count + k]
        decode_into(codes_ref, table_ref, weight_ref, block)


def decode_into(codes_ref, table_ref, weight_ref, block):
    words_all, columns = codes_ref.shape[-2:]
    lead = (0,) * (len(codes_ref.shape) - 2)
    for c in range(columns // LANES):
        lanes = pl.ds(c * LANES, LANES)
        low = table_ref[0:8, lanes]
        high = table_ref[8:16, lanes]
        for g in range(words_all // block):
            words = codes_ref[lead + (pl.ds(g * block, block), lanes)]
            words16 = words.astype(jnp.int16)
            for place in range(4):
                weight_ref[lead + (pl.ds((4 * g + place) * block, block), lanes)] = decode_tile(
                    words, words16, low, high, place
                )


def decode_cost(weights):
    return pl.CostEstimate(flops=8 * weights, bytes_accessed=3 * weights, transcendentals=0)


def decode_taps(core, codes, table, weights, start, stop):
    words, channels = codes.shape[1:]
    half = channels // 2
    into = [] if weights is None else [weights]
    return pl.pallas_call(
        lambda core_ref, codes_ref, table_ref, *refs: decode_into(codes_ref, table_ref, refs[-1], 64),
        grid_spec=pltpu.PrefetchScalarGridSpec(
            num_scalar_prefetch=1,
            grid=(stop - start,),
            in_specs=[
                pl.BlockSpec((1, words, half), lambda t, c: (start + t, 0, c[0])),
                pl.BlockSpec((16, half), lambda t, c: (0, c[0])),
            ]
            + [pl.BlockSpec(memory_space=pl.ANY)] * len(into),
            out_specs=pl.BlockSpec((1, 4 * words, half), lambda t, c: (start + t, 0, 0)),
        ),
        out_shape=jax.ShapeDtypeStruct((codes.shape[0], 4 * words, half), BF),
        input_output_aliases={3: 0} if into else {},
        compiler_params=params(34),
        cost_estimate=decode_cost((stop - start) * 4 * words * half),
    )(core, codes, table, *into)


def decode_columns(core, *pairs):
    count = len(pairs) // 2
    words, channels = pairs[0].shape
    half = channels // 2
    return pl.pallas_call(
        functools.partial(decode_kernel, count=count, block=64),
        grid_spec=pltpu.PrefetchScalarGridSpec(
            num_scalar_prefetch=1,
            grid=(1,),
            in_specs=[
                pl.BlockSpec((words, half), lambda t, c: (0, c[0])),
                pl.BlockSpec((16, half), lambda t, c: (0, c[0])),
            ]
            * count,
            out_specs=[pl.BlockSpec((4 * words, half), lambda t, c: (0, 0))] * count,
        ),
        out_shape=[jax.ShapeDtypeStruct((4 * words, half), BF)] * count,
        compiler_params=params(14),
        cost_estimate=decode_cost(count * 4 * words * half),
    )(core, *pairs)


def decode_rows(core, codes, table):
    words, channels = codes.shape
    half = words // 2
    return pl.pallas_call(
        functools.partial(decode_kernel, count=1, block=32),
        grid_spec=pltpu.PrefetchScalarGridSpec(
            num_scalar_prefetch=1,
            grid=(1,),
            in_specs=[
                pl.BlockSpec((half, channels), lambda t, c: (c[0], 0)),
                pl.BlockSpec((16, channels), lambda t, c: (0, 0)),
            ],
            out_specs=[pl.BlockSpec((4 * half, channels), lambda t, c: (0, 0))],
        ),
        out_shape=[jax.ShapeDtypeStruct((4 * half, channels), BF)],
        compiler_params=params(10),
        cost_estimate=decode_cost(4 * half * channels),
    )(core, codes, table)[0]


def conv_kernel(
    core_ref, sums_ref, mine_ref, theirs_ref, rim_mine_ref, rim_theirs_ref, gain_ref, shift_ref, bias_ref, time_ref,
    weight_ref, out_ref, act_ref, rim_ref, padded_ref, total_ref, *, members,
):
    tap = pl.program_id(0)
    taps = pl.num_programs(0)
    channels = gain_ref.shape[-1]
    height, across = mine_ref.shape[:2]
    cells = height * across
    core = core_ref[0]

    @pl.when(tap == 0)
    def _():
        parts = rim_theirs_ref[0:16, channels:].astype(F32)
        sums = sums_ref[...] + parts[0:2] + parts[2:4] + parts[4:6]
        sums = jnp.concatenate([sums, jnp.zeros((6, LANES), F32)], axis=0)
        spread = dot(sums, group_matrix(channels, True), precision=lax.Precision.HIGHEST)
        average = spread[0:1] / members
        mean_square = spread[1:2] / members
        scale = lax.rsqrt(mean_square - average * average + 1e-05) * gain_ref[...]
        offset = shift_ref[...] - average * scale
        size = 256
        matrix = shuffle_matrix(64)
        for side, ref in enumerate((mine_ref, theirs_ref)):
            for k in range(0, channels, size):
                lanes = slice(k, k + size)
                value = ref[:, :, lanes].reshape(cells, size).astype(F32)
                value = value * scale[:, lanes] + offset[:, lanes]
                value = (0.5 * value) * (1.0 + jnp.tanh(0.5 * value))
                act_ref[side, :, lanes] = dot(value.astype(BF), matrix)
        for side, ref in enumerate((rim_mine_ref, rim_theirs_ref)):
            for k in range(0, channels, size):
                lanes = slice(k, k + size)
                rim_ref[side, :, lanes] = dot(ref[:, lanes], matrix)

        column = iota((across, channels), 0)

        def spread_row(side, line, value, left, right):
            padded_ref[side, 0, line] = jnp.where(column == 0, left, pltpu.roll(value, 1, 0)).astype(BF)
            padded_ref[side, 1, line] = value.astype(BF)
            padded_ref[side, 2, line] = jnp.where(
                column == across - 1, right, pltpu.roll(value, across - 1, 0)
            ).astype(BF)

        for side in range(2):
            other = 1 - side
            is_left = core == side
            for line, base in ((0, 0), (height + 1, 2 * across)):
                corner = across + (height - 1 if line == 0 else 0)
                far = rim_ref[side, base + corner : base + corner + 1]
                next_last = rim_ref[other, base + across - 1 : base + across]
                next_first = rim_ref[other, base : base + 1]
                value = rim_ref[side, base : base + across]
                spread_row(
                    side, line, value, jnp.where(is_left, far, next_last), jnp.where(is_left, next_first, far)
                )
            outer_at = 4 * across
            inner_at = 4 * across + height

            @pl.loop(0, height)
            def _(r):
                outer = rim_ref[side, pl.ds(outer_at + r, 1)]
                inner = rim_ref[other, pl.ds(inner_at + r, 1)]
                value = act_ref[side, pl.ds(pl.multiple_of(r * across, across), across)]
                spread_row(
                    side, r + 1, value, jnp.where(is_left, outer, inner), jnp.where(is_left, inner, outer)
                )

    row_start = tap // 3
    col_start = tap % 3
    source = padded_ref[:, col_start, pl.ds(row_start, height)].reshape(2 * cells, channels)
    part = dot(source, weight_ref[0])

    @pl.when(tap == 0)
    def _():
        total_ref[...] = part

    @pl.when((tap > 0) & (tap < taps - 1))
    def _():
        total_ref[...] += part

    @pl.when(tap == taps - 1)
    def _():
        extra = bias_ref[...] + time_ref[0:1]
        half = channels // 2
        for side, ref in enumerate((mine_ref, theirs_ref)):
            image = jnp.where(core == 0, ref[:, :, :half], ref[:, :, half:]).reshape(cells, half).astype(F32)
            rows = slice(side * cells, (side + 1) * cells)
            conv = total_ref[rows] + part[rows] + extra
            out_ref[rows] = (image + conv).astype(BF)


def convolve(core, sums, mine, theirs, rim_mine, rim_theirs, gain, shift, bias, time_shift, weights, members):
    height, across, channels = mine.shape
    cells = height * across
    half = channels // 2
    whole = lambda *shape: pl.BlockSpec(shape, lambda t, c: (0,) * len(shape))
    part = lambda *shape: pl.BlockSpec(shape, lambda t, c: (0,) * (len(shape) - 1) + (c[0],))
    rim_rows = rim_mine.shape[0]
    return pl.pallas_call(
        functools.partial(conv_kernel, members=members),
        grid_spec=pltpu.PrefetchScalarGridSpec(
            num_scalar_prefetch=1,
            grid=(9,),
            in_specs=[
                whole(2, LANES),
                whole(height, across, channels),
                whole(height, across, channels),
                whole(rim_rows, channels),
                whole(rim_rows, channels + LANES),
                whole(1, channels),
                whole(1, channels),
                part(1, half),
                part(8, half),
                pl.BlockSpec((1, channels, half), lambda t, c: (t, 0, 0)),
            ],
            out_specs=whole(2 * cells, half),
            scratch_shapes=[
                pltpu.VMEM((2, cells, channels), F32),
                pltpu.VMEM((2, rim_rows, channels), F32),
                pltpu.VMEM((2, 3, height + 2, across, channels), BF),
                pltpu.VMEM((2 * cells, half), F32),
            ],
        ),
        out_shape=jax.ShapeDtypeStruct((2 * cells, half), BF),
        compiler_params=params(24),
    )(core, sums, mine, theirs, rim_mine, rim_theirs, gain, shift, bias, time_shift, weights)


def stale_kernel(near_ref, key_ref, value_ref, keys_ref, values_ref):
    keys_ref[...] = dot(near_ref[...], key_ref[...]).astype(BF)
    values_ref[...] = dot(near_ref[...], value_ref[...]).astype(BF)


def stale_pass(near, key_weight, value_weight):
    rows, channels = near.shape
    half = key_weight.shape[1]
    whole = pl.BlockSpec(memory_space=pltpu.VMEM)
    return pl.pallas_call(
        stale_kernel,
        in_specs=[whole] * 3,
        out_specs=[whole] * 2,
        out_shape=[jax.ShapeDtypeStruct((rows, half), BF)] * 2,
        compiler_params=params(16),
        cost_estimate=pl.CostEstimate(
            flops=4 * rows * channels * half, bytes_accessed=4 * channels * half, transcendentals=0
        ),
    )(near, key_weight, value_weight)


def attention_kernel(
    core_ref, mine_ref, theirs_ref, gain_ref, query_ref, key_ref, value_ref, near_keys_ref, near_values_ref,
    far_ref, out_weight_ref, send_ref, keep_ref, normed_ref, q_ref, k_ref, v_ref, mixed_ref, stale_keys_ref, stale_values_ref,
):
    rows, half = mine_ref.shape
    cells = rows // 2
    channels = 2 * half
    first = core_ref[0] == 0
    matrix = shuffle_matrix(64)
    for side in range(2):
        own = mine_ref[side * cells : (side + 1) * cells].astype(F32)
        other = theirs_ref[(1 - side) * cells : (2 - side) * cells].astype(F32)
        low = jnp.where(first, own, other)
        high = jnp.where(first, other, own)
        residual = jnp.concatenate([low, high], axis=1)
        if side == 0:
            keep_ref[...] = residual
        average = jnp.sum(residual, axis=1, keepdims=True) / channels
        centred = residual - average
        deviation = jnp.sum(centred * centred, axis=1, keepdims=True) / channels
        normed = (centred * lax.rsqrt(deviation + 1e-05) * gain_ref[...]).astype(BF)
        for k in range(0, channels, 256):
            normed_ref[side * cells : (side + 1) * cells, k : k + 256] = dot(
                normed[:, k : k + 256], matrix
            ).astype(BF)
    near_rows = near_keys_ref.shape[0]
    stale_keys_ref[:near_rows] = near_keys_ref[...]
    stale_values_ref[:near_rows] = near_values_ref[...]
    stale_keys_ref[near_rows:] = dot(far_ref[...], key_ref[...]).astype(BF)
    stale_values_ref[near_rows:] = dot(far_ref[...], value_ref[...]).astype(BF)
    normed = normed_ref[...]
    q_ref[...] = (dot(normed, query_ref[...]).astype(BF) * BF(1.0 / math.sqrt(HEAD_DIM))).astype(BF)
    k_ref[...] = dot(normed, key_ref[...]).astype(BF)
    v_ref[...] = dot(normed, value_ref[...]).astype(BF)

    ones = jnp.ones((cells, LANES), BF)
    stale_ones = jnp.ones((stale_keys_ref.shape[0], LANES), BF)
    lane = iota((cells, LANES), 1)
    for side in range(2):
        at = slice(side * cells, (side + 1) * cells)
        for pair in range(half // LANES):
            lanes = slice(pair * LANES, (pair + 1) * LANES)
            q = q_ref[at, lanes]
            zero = jnp.zeros_like(q)
            stacked = jnp.concatenate(
                [jnp.where(lane < HEAD_DIM, q, zero), jnp.where(lane < HEAD_DIM, zero, q)], axis=0
            )
            fresh = dot_t(stacked, k_ref[at, lanes])
            stale = dot_t(stacked, stale_keys_ref[:, lanes])
            highest = jnp.maximum(
                jnp.max(fresh, axis=1, keepdims=True), jnp.max(stale, axis=1, keepdims=True)
            )
            fresh = jnp.exp(fresh - highest).astype(BF)
            stale = jnp.exp(stale - highest).astype(BF)
            mixed = dot(fresh, jnp.concatenate([v_ref[at, lanes], ones], axis=1))
            mixed += dot(stale, jnp.concatenate([stale_values_ref[:, lanes], stale_ones], axis=1))
            mixed = mixed[:, :LANES] / mixed[:, LANES:]
            mixed_ref[at, lanes] = jnp.where(lane < HEAD_DIM, mixed[:cells], mixed[cells:]).astype(BF)
    mixture = shuffle(mixed_ref[...], 32).astype(BF)
    send_ref[...] = dot(mixture[cells:], out_weight_ref[...]).astype(BF)
    keep_ref[...] += dot(mixture[:cells], out_weight_ref[...])


def attention_pass(core, mine, theirs, gain, query, key, value, near_keys, near_values, far, out_weight):
    rows, half = mine.shape
    channels = 2 * half
    cells = rows // 2
    whole = pl.BlockSpec(memory_space=pltpu.VMEM)
    small = pl.BlockSpec(memory_space=pltpu.SMEM)
    return pl.pallas_call(
        attention_kernel,
        in_specs=[small] + [whole] * 10,
        out_specs=[whole] * 2,
        out_shape=[
            jax.ShapeDtypeStruct((cells, channels), BF),
            jax.ShapeDtypeStruct((cells, channels), F32),
        ],
        scratch_shapes=[
            pltpu.VMEM((rows, channels), BF),
            pltpu.VMEM((rows, half), BF),
            pltpu.VMEM((rows, half), BF),
            pltpu.VMEM((rows, half), BF),
            pltpu.VMEM((rows, half), BF),
            pltpu.VMEM((2 * far.shape[0], half), BF),
            pltpu.VMEM((2 * far.shape[0], half), BF),
        ],
        compiler_params=params(28),
    )(core, mine, theirs, gain, query, key, value, near_keys, near_values, far, out_weight)


def swap(values, axis, step):
    count = lax.axis_size(axis)
    return lax.ppermute(values, axis, [(i, i ^ step) for i in range(count)])


def steps_over(axis, first):
    count = lax.axis_size(axis)
    return [(axis, 2 * m - 1) for m in (1 << k for k in range(count.bit_length() - 1)) if m >= first]


def split_sums(sums):
    high = lax.reduce_precision(sums, 8, 7)
    rest = sums - high
    middle = lax.reduce_precision(rest, 8, 7)
    low = rest - middle
    parts = jnp.concatenate([high, middle, low, jnp.zeros((10, LANES), F32)])
    return parts.astype(BF)


def join_sums(parts):
    parts = parts.astype(F32)
    return parts[0:2] + parts[2:4] + parts[4:6]


def tie(first, second):
    return lax.optimization_barrier((first, second))


def on_device(
    image,
    stale_first,
    stale_normed,
    timestep,
    time_weight,
    gain_first,
    shift_first,
    codes_first,
    table_first,
    bias_first,
    attn_gain,
    query_codes,
    query_table,
    key_codes,
    key_table,
    value_codes,
    value_table,
    out_codes,
    out_table,
):
    height, across, channels = image.shape
    cells = height * across
    rows = lax.axis_size("row")
    cols = lax.axis_size("col")
    members = cells * rows * cols * (channels // GROUPS)
    core = (lax.axis_index("col") % 2).astype(jnp.int32)[None]

    sums, edges, pooled, time_shift = first_pass(core, timestep, image, stale_first, stale_normed, time_weight)

    row_at = lax.axis_index("row")
    col_at = lax.axis_index("col")
    beside = jnp.where(core[0] == 0, col_at - 1, col_at + 1)
    hops = steps_over("col", 2) + steps_over("row", 1)
    chunks = [(0, 2), (2, 6), (6, 9)]
    outer = jnp.zeros_like(edges[0])
    above = below = jnp.zeros((height + across, channels), BF)
    near = pooled
    weights = None
    codes = codes_first
    for at, (axis, step) in enumerate(hops):
        last = at == len(hops) - 1
        if weights is not None:
            (sums, near), weights = tie((sums, near), weights)
        if axis == "col":
            border = edges[0]
        else:
            partner = row_at ^ step
            border = jnp.concatenate([jnp.where(partner > row_at, edges[3], edges[2]), outer])
        parts = jnp.pad(split_sums(sums), ((0, border.shape[0] - across), (0, 0)))
        border = jnp.concatenate([border, parts], axis=1)
        if last:
            got_border = swap(border, axis, step)
            final = (near, axis, step)
        else:
            payload = jnp.concatenate([border, jnp.pad(near, ((0, 0), (0, LANES)))])
            got = swap(payload, axis, step)
            got_border = got[: border.shape[0]]
        if at == 1:
            partner_image = swap(image, "col", 1)
        if at < len(chunks):
            _, codes = tie((sums, near), codes)
            weights = decode_taps(core, codes, table_first, weights, *chunks[at])
        elif at == len(chunks):
            _, (query_codes, key_codes, value_codes) = tie(
                (sums, near), (query_codes, key_codes, value_codes)
            )
            query, key, value = decode_columns(
                core, query_codes, query_table, key_codes, key_table, value_codes, value_table
            )
            weights, key = tie(weights, key)
        sums = sums + join_sums(got_border[:across, channels:])
        cells_got = got_border[:, :channels]
        if axis == "col":
            outer = jnp.where((col_at ^ step) == beside, cells_got, outer)
        else:
            above = jnp.where(partner == row_at - 1, cells_got, above)
            below = jnp.where(partner == row_at + 1, cells_got, below)
        if not last:
            near = jnp.concatenate([near, got[border.shape[0] :, :channels]])
    (above, below, sums), weights = tie((above, below, sums), weights)
    rim = jnp.concatenate([above, below, outer, edges[1]])
    parts = jnp.pad(split_sums(sums), ((0, rim.shape[0] - across), (0, 0)))
    partner_rim = swap(jnp.concatenate([rim, parts], axis=1), "col", 1)
    near = jnp.concatenate([near, swap(*final)])

    residual = convolve(
        core, sums, image, partner_image, rim, partner_rim, gain_first[None], shift_first[None],
        bias_first[None], time_shift, weights, members,
    )
    (residual, near, out_codes), _ = tie((residual, near, out_codes), residual)
    partner_residual = swap(residual, "col", 1)
    far = swap(near, "col", 1)
    out_weight = decode_rows(core, out_codes, out_table)
    near_keys, near_values = stale_pass(near, key, value)
    send, keep = attention_pass(
        core, residual, partner_residual, attn_gain[None], query, key, value, near_keys, near_values, far, out_weight
    )
    output = keep + swap(send, "col", 1).astype(F32)
    return output.astype(BF).reshape(height, across, channels)


def solution(mesh):
    split = P("row", "col", None)
    in_specs = (split,) * 3 + (P(),) * 16
    return jax.shard_map(on_device, mesh=mesh, in_specs=in_specs, out_specs=split, check_vma=False)
```

```python
import functools
import math

import jax
import jax.numpy as jnp
from jax import lax
from jax.experimental import pallas as pl
from jax.experimental.pallas import tpu as pltpu
from jax.sharding import PartitionSpec as P

HEAD_DIM = 64
GROUPS = 32
TEMB = 320
POOL = 4
LANES = 128
BF = jnp.bfloat16
F32 = jnp.float32


def params(mebibytes):
    return pltpu.CompilerParams(vmem_limit_bytes=mebibytes * 2**20)


def dot(a, b, **extra):
    return jnp.dot(a, b, preferred_element_type=F32, **extra)


def dot_t(a, b):
    return lax.dot_general(a, b, (((1,), (1,)), ((), ())), preferred_element_type=F32)


def from_hbm(values):
    return pltpu.with_memory_space_constraint(values, pltpu.HBM)


def whole_block(shape):
    return pl.BlockSpec(shape, lambda *at: (0,) * len(shape))


def iota(shape, dim):
    return lax.broadcasted_iota(jnp.int32, shape, dim)


def shuffle_matrix(words):
    size = 4 * words
    row = iota((size, size), 0)
    col = iota((size, size), 1)
    return (row == 4 * (col % words) + col // words).astype(F32).astype(BF)


def shuffle(values, words):
    size = 4 * words
    matrix = shuffle_matrix(words)
    return jnp.concatenate(
        [dot(values[:, k : k + size], matrix) for k in range(0, values.shape[1], size)], axis=1
    )


def group_matrix(channels, transposed):
    members = channels // GROUPS
    shape = (LANES, channels) if transposed else (channels, LANES)
    channel = iota(shape, 1 if transposed else 0)
    group = iota(shape, 0 if transposed else 1)
    return ((channel >= group * members) & (channel < (group + 1) * members)).astype(F32)


def first_kernel(core_ref, step_ref, image_ref, first_ref, normed_ref, time_ref, sums_ref, edge_ref, pool_ref, shift_ref):
    channels = image_ref.shape[-1]
    height, across = first_ref.shape[:2]
    cells = height * across
    core = core_ref[0]
    image = image_ref[...].reshape(cells, channels).astype(F32)
    sums = jnp.sum(image, axis=0, keepdims=True)
    squares = jnp.sum(image * image, axis=0, keepdims=True)
    row8 = iota((8, channels), 0)
    both = jnp.where(row8 == 0, sums, jnp.where(row8 == 1, squares, 0.0))
    sums_ref[...] = dot(both, group_matrix(channels, False), precision=lax.Precision.HIGHEST)[0:2]

    cells_first = first_ref[...].reshape(cells, channels)
    row = iota((height, cells), 0)
    cell = iota((height, cells), 1)
    outer = jnp.where(core == 0, 0, across - 1)
    pick_outer = (cell == row * across + outer).astype(F32).astype(BF)
    pick_inner = (cell == row * across + (across - 1 - outer)).astype(F32).astype(BF)
    edge_ref[0] = dot(pick_outer, cells_first).astype(BF)
    edge_ref[1] = dot(pick_inner, cells_first).astype(BF)
    edge_ref[2] = first_ref[0]
    edge_ref[3] = first_ref[height - 1]

    pools = pool_ref.shape[0]
    pool = iota((pools, cells), 0)
    cell = iota((pools, cells), 1)
    in_row = cell // across // POOL == pool // (across // POOL)
    in_col = cell % across // POOL == pool % (across // POOL)
    average = jnp.where(in_row & in_col, 1.0 / (POOL * POOL), 0.0).astype(BF)
    pooled = dot(average, normed_ref[...].reshape(cells, channels)).astype(BF)
    pool_ref[...] = shuffle(pooled, 64).astype(BF)

    half = TEMB // 2
    place = iota((8, TEMB), 1)
    index = jnp.where(place < half, place, place - half).astype(F32)
    frequency = jnp.exp(-math.log(10000.0) * index / half)
    angle = step_ref[0].astype(F32) * frequency
    sinusoid = jnp.where(place < half, jnp.cos(angle), jnp.sin(angle)).astype(BF)
    shift = dot(sinusoid, time_ref[...])
    shift_ref[...] = shift * jax.nn.sigmoid(shift)


def first_pass(core, timestep, image, stale_first, stale_normed, time_weight):
    height, across, channels = image.shape
    pools = (height // POOL) * (across // POOL)
    small = pl.BlockSpec(memory_space=pltpu.SMEM)
    big = [from_hbm(x) for x in (image, stale_first, stale_normed, time_weight)]
    shapes = [(2, LANES), (4, height, channels), (pools, channels), (8, channels)]
    return pl.pallas_call(
        first_kernel,
        grid=(1,),
        in_specs=[small, small] + [whole_block(x.shape) for x in (image, stale_first, stale_normed, time_weight)],
        out_specs=[whole_block(shape) for shape in shapes],
        out_shape=[jax.ShapeDtypeStruct(shape, kind) for shape, kind in zip(shapes, (F32, BF, BF, F32))],
        compiler_params=params(16),
    )(core, timestep, *big)


def decode_tile(words, words16, low, high, place):
    lows = []
    highs = []
    for k in range(0, words.shape[0], 8):
        index = words[k : k + 8]
        if place:
            index = index >> (4 * place)
        index = index & 7
        lows.append(jnp.take_along_axis(low, index, axis=0, mode="promise_in_bounds"))
        highs.append(jnp.take_along_axis(high, index, axis=0, mode="promise_in_bounds"))
    bit = 4 * place + 3
    upper = (words16 & jnp.int16(1 << bit if bit < 15 else -(1 << 15))) != 0
    return jnp.where(
        upper, jnp.concatenate(highs, axis=0).astype(BF), jnp.concatenate(lows, axis=0).astype(BF)
    )


def decode_lanes(codes_ref, low, high, weight_ref, block):
    for g in range(codes_ref.shape[0] // block):
        words = codes_ref[g * block : (g + 1) * block]
        words16 = words.astype(jnp.int16)
        for place in range(4):
            at = (4 * g + place) * block
            weight_ref[at : at + block] = decode_tile(words, words16, low, high, place)


def lanes_at(index):
    return pl.ds(index * LANES, LANES)


def decode_cost(weights):
    return pl.CostEstimate(flops=8 * weights, bytes_accessed=3 * weights, transcendentals=0)


def taps_kernel(core_ref, token_ref, table_ref, codes_ref, *refs, start, count):
    weight_ref, token_out_ref, words_ref, held_ref, came, went = refs[-6:]
    slots = words_ref.shape[0]
    blocks = words_ref.shape[2] // LANES
    first = core_ref[0] * blocks
    token_out_ref[...] = token_ref[...]

    def far_lanes(block):
        return pl.ds(pl.multiple_of((first + block) * LANES, LANES), LANES)

    def fetch(tap, block):
        slot = tap % slots
        return pltpu.make_async_copy(
            codes_ref.at[start + tap, :, far_lanes(block)],
            words_ref.at[slot, :, lanes_at(block)],
            came.at[slot, block],
        )

    def store(tap, block):
        slot = tap % 2
        return pltpu.make_async_copy(
            held_ref.at[slot, :, lanes_at(block)],
            weight_ref.at[start + tap, :, lanes_at(block)],
            went.at[slot, block],
        )

    for tap in range(min(slots, count)):
        for block in range(blocks):
            fetch(tap, block).start()

    @pl.loop(0, count)
    def _(tap):
        for block in range(blocks):
            fetch(tap, block).wait()

            @pl.when(tap >= 2)
            def _():
                store(tap - 2, block).wait()

            decode_lanes(
                words_ref.at[tap % slots, :, lanes_at(block)],
                table_ref[0:8, far_lanes(block)],
                table_ref[8:16, far_lanes(block)],
                held_ref.at[tap % 2, :, lanes_at(block)],
                64,
            )
            store(tap, block).start()

            @pl.when(tap + slots < count)
            def _():
                fetch(tap + slots, block).start()

    for tap in range(max(count - 2, 0), count):
        for block in range(blocks):
            store(tap, block).wait()


def decode_taps(core, token, codes, table, weights, start, stop):
    words, channels = codes.shape[1:]
    half = channels // 2
    count = stop - start
    into = [] if weights is None else [from_hbm(weights)]
    whole = pl.BlockSpec(memory_space=pltpu.VMEM)
    far = pl.BlockSpec(memory_space=pl.ANY)
    return pl.pallas_call(
        functools.partial(taps_kernel, start=start, count=count),
        in_specs=[pl.BlockSpec(memory_space=pltpu.SMEM), whole, whole, far] + [far] * len(into),
        out_specs=[far, whole],
        out_shape=[
            pltpu.HBM((codes.shape[0], 4 * words, half), BF),
            jax.ShapeDtypeStruct(token.shape, token.dtype),
        ],
        scratch_shapes=[
            pltpu.VMEM((3, words, half), jnp.int32),
            pltpu.VMEM((2, 4 * words, half), BF),
            pltpu.SemaphoreType.DMA((3, half // LANES)),
            pltpu.SemaphoreType.DMA((2, half // LANES)),
        ],
        input_output_aliases={4: 0} if into else {},
        compiler_params=params(10),
        cost_estimate=decode_cost(count * 4 * words * half),
    )(core, token, table, from_hbm(codes), *into)


def matrices_kernel(core_ref, token_ref, *refs, count, by_rows, block):
    tables = refs[:count]
    codes = refs[count : 2 * count]
    weights = refs[2 * count : 3 * count]
    token_out_ref, words_ref, came = refs[3 * count :]
    token_out_ref[...] = token_ref[...]
    rows = words_ref.shape[1]
    blocks = words_ref.shape[2] // LANES
    core = core_ref[0]
    first = 0 if by_rows else core * blocks
    row = pl.multiple_of(core * rows, 8) if by_rows else 0

    def far_lanes(at):
        return lanes_at(at) if by_rows else pl.ds(pl.multiple_of((first + at) * LANES, LANES), LANES)

    def fetch(k, at):
        return pltpu.make_async_copy(
            codes[k].at[pl.ds(row, rows), far_lanes(at)], words_ref.at[k, :, lanes_at(at)], came.at[k, at]
        )

    for k in range(count):
        for at in range(blocks):
            fetch(k, at).start()
    for k in range(count):
        for at in range(blocks):
            fetch(k, at).wait()
            decode_lanes(
                words_ref.at[k, :, lanes_at(at)],
                tables[k][0:8, far_lanes(at)],
                tables[k][8:16, far_lanes(at)],
                weights[k].at[:, lanes_at(at)],
                block,
            )


def decode_matrices(core, token, codes, tables, by_rows):
    count = len(codes)
    words, channels = codes[0].shape
    rows, columns = (words // 2, channels) if by_rows else (words, channels // 2)
    whole = pl.BlockSpec(memory_space=pltpu.VMEM)
    return pl.pallas_call(
        functools.partial(matrices_kernel, count=count, by_rows=by_rows, block=32 if by_rows else 64),
        in_specs=[pl.BlockSpec(memory_space=pltpu.SMEM)]
        + [whole] * (1 + count)
        + [pl.BlockSpec(memory_space=pl.ANY)] * count,
        out_specs=[whole] * (count + 1),
        out_shape=[jax.ShapeDtypeStruct((4 * rows, columns), BF)] * count
        + [jax.ShapeDtypeStruct(token.shape, token.dtype)],
        scratch_shapes=[
            pltpu.VMEM((count, rows, columns), jnp.int32),
            pltpu.SemaphoreType.DMA((count, columns // LANES)),
        ],
        compiler_params=params(10),
        cost_estimate=decode_cost(count * 4 * rows * columns),
    )(core, token, *tables, *[from_hbm(x) for x in codes])


def conv_kernel(
    core_ref, sums_ref, mine_ref, theirs_ref, rim_mine_ref, rim_theirs_ref, gain_ref, shift_ref, bias_ref, time_ref,
    weight_ref, out_ref, act_ref, rim_ref, padded_ref, total_ref, held_ref, arrived, *, members,
):
    taps = weight_ref.shape[0]
    slots = held_ref.shape[0]

    def fetch(tap):
        slot = tap % slots
        return pltpu.make_async_copy(weight_ref.at[tap], held_ref.at[slot], arrived.at[slot])

    for tap in range(slots):
        fetch(tap).start()
    channels = gain_ref.shape[-1]
    height, across = mine_ref.shape[:2]
    cells = height * across
    core = core_ref[0]

    parts = rim_theirs_ref[0:16, channels:].astype(F32)
    sums = sums_ref[...] + parts[0:2] + parts[2:4] + parts[4:6]
    sums = jnp.concatenate([sums, jnp.zeros((6, LANES), F32)], axis=0)
    spread = dot(sums, group_matrix(channels, True), precision=lax.Precision.HIGHEST)
    average = spread[0:1] / members
    mean_square = spread[1:2] / members
    scale = lax.rsqrt(mean_square - average * average + 1e-05) * gain_ref[...]
    offset = shift_ref[...] - average * scale
    size = 256
    matrix = shuffle_matrix(64)
    for side, ref in enumerate((mine_ref, theirs_ref)):
        for k in range(0, channels, size):
            lanes = slice(k, k + size)
            value = ref[:, :, lanes].reshape(cells, size).astype(F32)
            value = value * scale[:, lanes] + offset[:, lanes]
            value = (0.5 * value) * (1.0 + jnp.tanh(0.5 * value))
            act_ref[side, :, lanes] = dot(value.astype(BF), matrix)
    for side, ref in enumerate((rim_mine_ref, rim_theirs_ref)):
        for k in range(0, channels, size):
            lanes = slice(k, k + size)
            rim_ref[side, :, lanes] = dot(ref[:, lanes], matrix)

    column = iota((across, channels), 0)

    def spread_row(side, line, value, left, right):
        padded_ref[side, 0, line] = jnp.where(column == 0, left, pltpu.roll(value, 1, 0)).astype(BF)
        padded_ref[side, 1, line] = value.astype(BF)
        padded_ref[side, 2, line] = jnp.where(
            column == across - 1, right, pltpu.roll(value, across - 1, 0)
        ).astype(BF)

    for side in range(2):
        other = 1 - side
        is_left = core == side
        for line, base in ((0, 0), (height + 1, 2 * across)):
            corner = across + (height - 1 if line == 0 else 0)
            far = rim_ref[side, base + corner : base + corner + 1]
            next_last = rim_ref[other, base + across - 1 : base + across]
            next_first = rim_ref[other, base : base + 1]
            value = rim_ref[side, base : base + across]
            spread_row(
                side, line, value, jnp.where(is_left, far, next_last), jnp.where(is_left, next_first, far)
            )
        outer_at = 4 * across
        inner_at = 4 * across + height

        @pl.loop(0, height, unroll=4)
        def _(r):
            outer = rim_ref[side, pl.ds(outer_at + r, 1)]
            inner = rim_ref[other, pl.ds(inner_at + r, 1)]
            value = act_ref[side, pl.ds(pl.multiple_of(r * across, across), across)]
            spread_row(
                side, r + 1, value, jnp.where(is_left, outer, inner), jnp.where(is_left, inner, outer)
            )

    half = channels // 2

    def tap_product(tap):
        fetch(tap).wait()
        source = padded_ref[:, tap % 3, pl.ds(tap // 3, height)].reshape(2 * cells, channels)
        return dot(source, held_ref[tap % slots])

    total_ref[...] = tap_product(0)
    fetch(slots).start()

    @pl.loop(1, taps - slots)
    def _(tap):
        total_ref[...] += tap_product(tap)
        fetch(tap + slots).start()

    for tap in range(taps - slots, taps - 1):
        total_ref[...] += tap_product(tap)
    last = tap_product(taps - 1)
    extra = bias_ref[...] + time_ref[0:1]
    extra = jnp.where(core == 0, extra[:, :half], extra[:, half:])
    for side, ref in enumerate((mine_ref, theirs_ref)):
        image = jnp.where(core == 0, ref[:, :, :half], ref[:, :, half:]).reshape(cells, half).astype(F32)
        rows = slice(side * cells, (side + 1) * cells)
        out_ref[rows] = (image + (total_ref[rows] + last[rows] + extra)).astype(BF)


def convolve(core, sums, mine, theirs, rim_mine, rim_theirs, gain, shift, bias, time_shift, weights, members):
    height, across, channels = mine.shape
    cells = height * across
    half = channels // 2
    whole = pl.BlockSpec(memory_space=pltpu.VMEM)
    small = pl.BlockSpec(memory_space=pltpu.SMEM)
    rim_rows = rim_mine.shape[0]
    return pl.pallas_call(
        functools.partial(conv_kernel, members=members),
        in_specs=[small] + [whole] * 9 + [pl.BlockSpec(memory_space=pl.ANY)],
        out_specs=whole,
        out_shape=jax.ShapeDtypeStruct((2 * cells, half), BF),
        scratch_shapes=[
            pltpu.VMEM((2, cells, channels), F32),
            pltpu.VMEM((2, rim_rows, channels), F32),
            pltpu.VMEM((2, 3, height + 2, across, channels), BF),
            pltpu.VMEM((2 * cells, half), F32),
            pltpu.VMEM((3, channels, half), BF),
            pltpu.SemaphoreType.DMA((3,)),
        ],
        compiler_params=params(26),
        cost_estimate=pl.CostEstimate(
            flops=36 * cells * channels * half, bytes_accessed=18 * channels * half, transcendentals=2 * cells * channels
        ),
    )(core, sums, mine, theirs, rim_mine, rim_theirs, gain, shift, bias, time_shift, from_hbm(weights))


def stale_kernel(near_ref, key_ref, value_ref, keys_ref, values_ref):
    keys_ref[...] = dot(near_ref[...], key_ref[...]).astype(BF)
    values_ref[...] = dot(near_ref[...], value_ref[...]).astype(BF)


def stale_pass(near, key_weight, value_weight):
    rows, channels = near.shape
    half = key_weight.shape[1]
    whole = pl.BlockSpec(memory_space=pltpu.VMEM)
    return pl.pallas_call(
        stale_kernel,
        in_specs=[whole] * 3,
        out_specs=[whole] * 2,
        out_shape=[jax.ShapeDtypeStruct((rows, half), BF)] * 2,
        compiler_params=params(16),
        cost_estimate=pl.CostEstimate(
            flops=4 * rows * channels * half, bytes_accessed=4 * channels * half, transcendentals=0
        ),
    )(near, key_weight, value_weight)


def attention_kernel(
    core_ref, mine_ref, theirs_ref, gain_ref, query_ref, key_ref, value_ref, near_keys_ref, near_values_ref,
    far_ref, out_weight_ref, send_ref, keep_ref, normed_ref, q_ref, k_ref, v_ref, mixed_ref, stale_keys_ref, stale_values_ref,
):
    rows, half = mine_ref.shape
    cells = rows // 2
    channels = 2 * half
    first = core_ref[0] == 0
    matrix = shuffle_matrix(64)
    for side in range(2):
        own = mine_ref[side * cells : (side + 1) * cells].astype(F32)
        other = theirs_ref[(1 - side) * cells : (2 - side) * cells].astype(F32)
        low = jnp.where(first, own, other)
        high = jnp.where(first, other, own)
        residual = jnp.concatenate([low, high], axis=1)
        if side == 0:
            keep_ref[...] = residual
        average = jnp.sum(residual, axis=1, keepdims=True) / channels
        centred = residual - average
        deviation = jnp.sum(centred * centred, axis=1, keepdims=True) / channels
        normed = (centred * lax.rsqrt(deviation + 1e-05) * gain_ref[...]).astype(BF)
        for k in range(0, channels, 256):
            normed_ref[side * cells : (side + 1) * cells, k : k + 256] = dot(
                normed[:, k : k + 256], matrix
            ).astype(BF)
    near_rows = near_keys_ref.shape[0]
    stale_keys_ref[:near_rows] = near_keys_ref[...]
    stale_values_ref[:near_rows] = near_values_ref[...]
    stale_keys_ref[near_rows:] = dot(far_ref[...], key_ref[...]).astype(BF)
    stale_values_ref[near_rows:] = dot(far_ref[...], value_ref[...]).astype(BF)
    normed = normed_ref[...]
    q_ref[...] = (dot(normed, query_ref[...]).astype(BF) * BF(1.0 / math.sqrt(HEAD_DIM))).astype(BF)
    k_ref[...] = dot(normed, key_ref[...]).astype(BF)
    v_ref[...] = dot(normed, value_ref[...]).astype(BF)

    ones = jnp.ones((cells, LANES), BF)
    stale_ones = jnp.ones((stale_keys_ref.shape[0], LANES), BF)
    lane = iota((cells, LANES), 1)
    for side in range(2):
        at = slice(side * cells, (side + 1) * cells)
        for pair in range(half // LANES):
            lanes = slice(pair * LANES, (pair + 1) * LANES)
            q = q_ref[at, lanes]
            zero = jnp.zeros_like(q)
            stacked = jnp.concatenate(
                [jnp.where(lane < HEAD_DIM, q, zero), jnp.where(lane < HEAD_DIM, zero, q)], axis=0
            )
            fresh = dot_t(stacked, k_ref[at, lanes])
            stale = dot_t(stacked, stale_keys_ref[:, lanes])
            highest = jnp.maximum(
                jnp.max(fresh, axis=1, keepdims=True), jnp.max(stale, axis=1, keepdims=True)
            )
            fresh = jnp.exp(fresh - highest).astype(BF)
            stale = jnp.exp(stale - highest).astype(BF)
            mixed = dot(fresh, jnp.concatenate([v_ref[at, lanes], ones], axis=1))
            mixed += dot(stale, jnp.concatenate([stale_values_ref[:, lanes], stale_ones], axis=1))
            mixed = mixed[:, :LANES] / mixed[:, LANES:]
            mixed_ref[at, lanes] = jnp.where(lane < HEAD_DIM, mixed[:cells], mixed[cells:]).astype(BF)
    mixture = shuffle(mixed_ref[...], 32).astype(BF)
    send_ref[...] = dot(mixture[cells:], out_weight_ref[...]).astype(BF)
    keep_ref[...] += dot(mixture[:cells], out_weight_ref[...])


def attention_pass(core, mine, theirs, gain, query, key, value, near_keys, near_values, far, out_weight):
    rows, half = mine.shape
    channels = 2 * half
    cells = rows // 2
    whole = pl.BlockSpec(memory_space=pltpu.VMEM)
    small = pl.BlockSpec(memory_space=pltpu.SMEM)
    return pl.pallas_call(
        attention_kernel,
        in_specs=[small] + [whole] * 10,
        out_specs=[whole] * 2,
        out_shape=[
            jax.ShapeDtypeStruct((cells, channels), BF),
            jax.ShapeDtypeStruct((cells, channels), F32),
        ],
        scratch_shapes=[
            pltpu.VMEM((rows, channels), BF),
            pltpu.VMEM((rows, half), BF),
            pltpu.VMEM((rows, half), BF),
            pltpu.VMEM((rows, half), BF),
            pltpu.VMEM((rows, half), BF),
            pltpu.VMEM((2 * far.shape[0], half), BF),
            pltpu.VMEM((2 * far.shape[0], half), BF),
        ],
        compiler_params=params(28),
    )(core, mine, theirs, gain, query, key, value, near_keys, near_values, far, out_weight)


def swap(values, axis, step):
    count = lax.axis_size(axis)
    return lax.ppermute(values, axis, [(i, i ^ step) for i in range(count)])


def steps_over(axis, first):
    count = lax.axis_size(axis)
    return [(axis, 2 * m - 1) for m in (1 << k for k in range(count.bit_length() - 1)) if m >= first]


def split_sums(sums):
    high = lax.reduce_precision(sums, 8, 7)
    rest = sums - high
    middle = lax.reduce_precision(rest, 8, 7)
    low = rest - middle
    parts = jnp.concatenate([high, middle, low, jnp.zeros((10, LANES), F32)])
    return parts.astype(BF)


def join_sums(parts):
    parts = parts.astype(F32)
    return parts[0:2] + parts[2:4] + parts[4:6]


def tie(first, second):
    return lax.optimization_barrier((first, second))


def on_device(
    image,
    stale_first,
    stale_normed,
    timestep,
    time_weight,
    gain_first,
    shift_first,
    codes_first,
    table_first,
    bias_first,
    attn_gain,
    query_codes,
    query_table,
    key_codes,
    key_table,
    value_codes,
    value_table,
    out_codes,
    out_table,
):
    height, across, channels = image.shape
    cells = height * across
    rows = lax.axis_size("row")
    cols = lax.axis_size("col")
    members = cells * rows * cols * (channels // GROUPS)
    core = (lax.axis_index("col") % 2).astype(jnp.int32)[None]

    sums, edges, pooled, time_shift = first_pass(core, timestep, image, stale_first, stale_normed, time_weight)

    row_at = lax.axis_index("row")
    col_at = lax.axis_index("col")
    beside = jnp.where(core[0] == 0, col_at - 1, col_at + 1)
    hops = steps_over("col", 2) + steps_over("row", 1)
    chunks = [(0, 2), (2, 6), (6, 9)]
    outer = jnp.zeros_like(edges[0])
    above = below = jnp.zeros((height + across, channels), BF)
    near = pooled
    weights = None
    token = sums
    for at, (axis, step) in enumerate(hops):
        last = at == len(hops) - 1
        (sums, near), token = tie((sums, near), token)
        if axis == "col":
            border = edges[0]
        else:
            partner = row_at ^ step
            border = jnp.concatenate([jnp.where(partner > row_at, edges[3], edges[2]), outer])
        parts = jnp.pad(split_sums(sums), ((0, border.shape[0] - across), (0, 0)))
        border = jnp.concatenate([border, parts], axis=1)
        if last:
            got_border = swap(border, axis, step)
            final = (near, axis, step)
        else:
            payload = jnp.concatenate([border, jnp.pad(near, ((0, 0), (0, LANES)))])
            got = swap(payload, axis, step)
            got_border = got[: border.shape[0]]
        if at == 1:
            partner_image = swap(image, "col", 1)
        if at < len(chunks):
            weights, token = decode_taps(core, token, codes_first, table_first, weights, *chunks[at])
        elif at == len(chunks):
            query, key, value, token = decode_matrices(
                core, token, (query_codes, key_codes, value_codes), (query_table, key_table, value_table), False
            )
        sums = sums + join_sums(got_border[:across, channels:])
        cells_got = got_border[:, :channels]
        if axis == "col":
            outer = jnp.where((col_at ^ step) == beside, cells_got, outer)
        else:
            above = jnp.where(partner == row_at - 1, cells_got, above)
            below = jnp.where(partner == row_at + 1, cells_got, below)
        if not last:
            near = jnp.concatenate([near, got[border.shape[0] :, :channels]])
    (above, below, sums), token = tie((above, below, sums), token)
    rim = jnp.concatenate([above, below, outer, edges[1]])
    parts = jnp.pad(split_sums(sums), ((0, rim.shape[0] - across), (0, 0)))
    partner_rim = swap(jnp.concatenate([rim, parts], axis=1), "col", 1)
    beyond = swap(*final)

    residual = convolve(
        core, sums, image, partner_image, rim, partner_rim, gain_first[None], shift_first[None],
        bias_first[None], time_shift, weights, members,
    )
    (residual, beyond), token = tie((residual, beyond), token)
    near = jnp.concatenate([near, beyond])
    partner_residual = swap(residual, "col", 1)
    far = swap(near, "col", 1)
    out_weight, _ = decode_matrices(core, token, (out_codes,), (out_table,), True)
    near_keys, near_values = stale_pass(near, key, value)
    send, keep = attention_pass(
        core, residual, partner_residual, attn_gain[None], query, key, value, near_keys, near_values, far, out_weight
    )
    output = keep + swap(send, "col", 1).astype(F32)
    return output.astype(BF).reshape(height, across, channels)


def solution(mesh):
    split = P("row", "col", None)
    in_specs = (split,) * 3 + (P(),) * 16
    return jax.shard_map(on_device, mesh=mesh, in_specs=in_specs, out_specs=split, check_vma=False)
```

```python
import functools
import math

import jax
import jax.numpy as jnp
from jax import lax
from jax.experimental import pallas as pl
from jax.experimental.pallas import tpu as pltpu
from jax.sharding import PartitionSpec as P

HEAD_DIM = 64
GROUPS = 32
TEMB = 320
POOL = 4
LANES = 128
BF = jnp.bfloat16
F32 = jnp.float32


def params(mebibytes):
    return pltpu.CompilerParams(vmem_limit_bytes=mebibytes * 2**20)


def dot(a, b, **extra):
    return jnp.dot(a, b, preferred_element_type=F32, **extra)


def dot_t(a, b):
    return lax.dot_general(a, b, (((1,), (1,)), ((), ())), preferred_element_type=F32)


def from_hbm(values):
    return pltpu.with_memory_space_constraint(values, pltpu.HBM)


def whole_block(shape):
    return pl.BlockSpec(shape, lambda *at: (0,) * len(shape))


def iota(shape, dim):
    return lax.broadcasted_iota(jnp.int32, shape, dim)


def shuffle_matrix(words):
    size = 4 * words
    row = iota((size, size), 0)
    col = iota((size, size), 1)
    return (row == 4 * (col % words) + col // words).astype(F32).astype(BF)


def shuffle(values, words):
    size = 4 * words
    matrix = shuffle_matrix(words)
    return jnp.concatenate(
        [dot(values[:, k : k + size], matrix) for k in range(0, values.shape[1], size)], axis=1
    )


def group_matrix(channels, transposed):
    members = channels // GROUPS
    shape = (LANES, channels) if transposed else (channels, LANES)
    channel = iota(shape, 1 if transposed else 0)
    group = iota(shape, 0 if transposed else 1)
    return ((channel >= group * members) & (channel < (group + 1) * members)).astype(F32)


def first_kernel(core_ref, step_ref, image_ref, first_ref, normed_ref, time_ref, sums_ref, edge_ref, pool_ref, shift_ref):
    channels = image_ref.shape[-1]
    height, across = first_ref.shape[:2]
    cells = height * across
    core = core_ref[0]
    image = image_ref[...].reshape(cells, channels).astype(F32)
    sums = jnp.sum(image, axis=0, keepdims=True)
    squares = jnp.sum(image * image, axis=0, keepdims=True)
    row8 = iota((8, channels), 0)
    both = jnp.where(row8 == 0, sums, jnp.where(row8 == 1, squares, 0.0))
    sums_ref[...] = dot(both, group_matrix(channels, False), precision=lax.Precision.HIGHEST)[0:2]

    cells_first = first_ref[...].reshape(cells, channels)
    row = iota((height, cells), 0)
    cell = iota((height, cells), 1)
    outer = jnp.where(core == 0, 0, across - 1)
    pick_outer = (cell == row * across + outer).astype(F32).astype(BF)
    pick_inner = (cell == row * across + (across - 1 - outer)).astype(F32).astype(BF)
    edge_ref[0] = dot(pick_outer, cells_first).astype(BF)
    edge_ref[1] = dot(pick_inner, cells_first).astype(BF)
    edge_ref[2] = first_ref[0]
    edge_ref[3] = first_ref[height - 1]

    pools = pool_ref.shape[0]
    pool = iota((pools, cells), 0)
    cell = iota((pools, cells), 1)
    in_row = cell // across // POOL == pool // (across // POOL)
    in_col = cell % across // POOL == pool % (across // POOL)
    average = jnp.where(in_row & in_col, 1.0 / (POOL * POOL), 0.0).astype(BF)
    pooled = dot(average, normed_ref[...].reshape(cells, channels)).astype(BF)
    pool_ref[...] = shuffle(pooled, 64).astype(BF)

    half = TEMB // 2
    place = iota((8, TEMB), 1)
    index = jnp.where(place < half, place, place - half).astype(F32)
    frequency = jnp.exp(-math.log(10000.0) * index / half)
    angle = step_ref[0].astype(F32) * frequency
    sinusoid = jnp.where(place < half, jnp.cos(angle), jnp.sin(angle)).astype(BF)
    shift = dot(sinusoid, time_ref[...])
    shift_ref[...] = shift * jax.nn.sigmoid(shift)


def first_pass(core, timestep, image, stale_first, stale_normed, time_weight):
    height, across, channels = image.shape
    pools = (height // POOL) * (across // POOL)
    small = pl.BlockSpec(memory_space=pltpu.SMEM)
    big = [from_hbm(x) for x in (image, stale_first, stale_normed, time_weight)]
    shapes = [(2, LANES), (4, height, channels), (pools, channels), (8, channels)]
    return pl.pallas_call(
        first_kernel,
        grid=(1,),
        in_specs=[small, small] + [whole_block(x.shape) for x in (image, stale_first, stale_normed, time_weight)],
        out_specs=[whole_block(shape) for shape in shapes],
        out_shape=[jax.ShapeDtypeStruct(shape, kind) for shape, kind in zip(shapes, (F32, BF, BF, F32))],
        compiler_params=params(16),
    )(core, timestep, *big)


def decode_tile(words, words16, low, high, place):
    lows = []
    highs = []
    for k in range(0, words.shape[0], 8):
        index = words[k : k + 8]
        if place:
            index = index >> (4 * place)
        index = index & 7
        lows.append(jnp.take_along_axis(low, index, axis=0, mode="promise_in_bounds"))
        highs.append(jnp.take_along_axis(high, index, axis=0, mode="promise_in_bounds"))
    bit = 4 * place + 3
    upper = (words16 & jnp.int16(1 << bit if bit < 15 else -(1 << 15))) != 0
    return jnp.where(
        upper, jnp.concatenate(highs, axis=0).astype(BF), jnp.concatenate(lows, axis=0).astype(BF)
    )


def decode_lanes(codes_ref, low, high, weight_ref, block):
    for g in range(codes_ref.shape[0] // block):
        words = codes_ref[g * block : (g + 1) * block]
        words16 = words.astype(jnp.int16)
        for place in range(4):
            at = (4 * g + place) * block
            weight_ref[at : at + block] = decode_tile(words, words16, low, high, place)


def lanes_at(index):
    return pl.ds(index * LANES, LANES)


def decode_cost(weights):
    return pl.CostEstimate(flops=8 * weights, bytes_accessed=3 * weights, transcendentals=0)


def taps_kernel(core_ref, token_ref, table_ref, codes_ref, *refs, start, count):
    weight_ref, token_out_ref, words_ref, held_ref, came, went = refs[-6:]
    slots = words_ref.shape[0]
    blocks = words_ref.shape[2] // LANES
    first = core_ref[0] * blocks
    token_out_ref[...] = token_ref[...]

    def far_lanes(block):
        return pl.ds(pl.multiple_of((first + block) * LANES, LANES), LANES)

    def fetch(tap, block):
        slot = tap % slots
        return pltpu.make_async_copy(
            codes_ref.at[start + tap, :, far_lanes(block)],
            words_ref.at[slot, :, lanes_at(block)],
            came.at[slot, block],
        )

    def store(tap, block):
        slot = tap % 2
        return pltpu.make_async_copy(
            held_ref.at[slot, :, lanes_at(block)],
            weight_ref.at[start + tap, :, lanes_at(block)],
            went.at[slot, block],
        )

    for tap in range(min(slots, count)):
        for block in range(blocks):
            fetch(tap, block).start()

    @pl.loop(0, count)
    def _(tap):
        for block in range(blocks):
            fetch(tap, block).wait()

            @pl.when(tap >= 2)
            def _():
                store(tap - 2, block).wait()

            decode_lanes(
                words_ref.at[tap % slots, :, lanes_at(block)],
                table_ref[0:8, far_lanes(block)],
                table_ref[8:16, far_lanes(block)],
                held_ref.at[tap % 2, :, lanes_at(block)],
                64,
            )
            store(tap, block).start()

            @pl.when(tap + slots < count)
            def _():
                fetch(tap + slots, block).start()

    for tap in range(max(count - 2, 0), count):
        for block in range(blocks):
            store(tap, block).wait()


def decode_taps(core, token, codes, table, weights, start, stop):
    words, channels = codes.shape[1:]
    half = channels // 2
    count = stop - start
    into = [] if weights is None else [from_hbm(weights)]
    whole = pl.BlockSpec(memory_space=pltpu.VMEM)
    far = pl.BlockSpec(memory_space=pl.ANY)
    return pl.pallas_call(
        functools.partial(taps_kernel, start=start, count=count),
        in_specs=[pl.BlockSpec(memory_space=pltpu.SMEM), whole, whole, far] + [far] * len(into),
        out_specs=[far, whole],
        out_shape=[
            pltpu.HBM((codes.shape[0], 4 * words, half), BF),
            jax.ShapeDtypeStruct(token.shape, token.dtype),
        ],
        scratch_shapes=[
            pltpu.VMEM((3, words, half), jnp.int32),
            pltpu.VMEM((2, 4 * words, half), BF),
            pltpu.SemaphoreType.DMA((3, half // LANES)),
            pltpu.SemaphoreType.DMA((2, half // LANES)),
        ],
        input_output_aliases={4: 0} if into else {},
        compiler_params=params(10),
        cost_estimate=decode_cost(count * 4 * words * half),
    )(core, token, table, from_hbm(codes), *into)


def matrices_kernel(core_ref, token_ref, *refs, count, by_rows, block):
    tables = refs[:count]
    codes = refs[count : 2 * count]
    weights = refs[2 * count : 3 * count]
    token_out_ref, words_ref, came = refs[3 * count :]
    token_out_ref[...] = token_ref[...]
    rows = words_ref.shape[1]
    blocks = words_ref.shape[2] // LANES
    core = core_ref[0]
    first = 0 if by_rows else core * blocks
    row = pl.multiple_of(core * rows, 8) if by_rows else 0

    def far_lanes(at):
        return lanes_at(at) if by_rows else pl.ds(pl.multiple_of((first + at) * LANES, LANES), LANES)

    def fetch(k, at):
        return pltpu.make_async_copy(
            codes[k].at[pl.ds(row, rows), far_lanes(at)], words_ref.at[k, :, lanes_at(at)], came.at[k, at]
        )

    for k in range(count):
        for at in range(blocks):
            fetch(k, at).start()
    for k in range(count):
        for at in range(blocks):
            fetch(k, at).wait()
            decode_lanes(
                words_ref.at[k, :, lanes_at(at)],
                tables[k][0:8, far_lanes(at)],
                tables[k][8:16, far_lanes(at)],
                weights[k].at[:, lanes_at(at)],
                block,
            )


def decode_matrices(core, token, codes, tables, by_rows):
    count = len(codes)
    words, channels = codes[0].shape
    rows, columns = (words // 2, channels) if by_rows else (words, channels // 2)
    whole = pl.BlockSpec(memory_space=pltpu.VMEM)
    return pl.pallas_call(
        functools.partial(matrices_kernel, count=count, by_rows=by_rows, block=32 if by_rows else 64),
        in_specs=[pl.BlockSpec(memory_space=pltpu.SMEM)]
        + [whole] * (1 + count)
        + [pl.BlockSpec(memory_space=pl.ANY)] * count,
        out_specs=[whole] * (count + 1),
        out_shape=[jax.ShapeDtypeStruct((4 * rows, columns), BF)] * count
        + [jax.ShapeDtypeStruct(token.shape, token.dtype)],
        scratch_shapes=[
            pltpu.VMEM((count, rows, columns), jnp.int32),
            pltpu.SemaphoreType.DMA((count, columns // LANES)),
        ],
        compiler_params=params(10),
        cost_estimate=decode_cost(count * 4 * rows * columns),
    )(core, token, *tables, *[from_hbm(x) for x in codes])


def conv_kernel(
    core_ref, sums_ref, mine_ref, theirs_ref, rim_mine_ref, rim_theirs_ref, gain_ref, shift_ref, bias_ref, time_ref,
    weight_ref, out_ref, act_ref, rim_ref, padded_ref, total_ref, held_ref, arrived, *, members,
):
    slots = held_ref.shape[0]

    def fetch(tap_row):
        slot = tap_row % slots
        return pltpu.make_async_copy(
            weight_ref.at[3 * tap_row : 3 * tap_row + 3], held_ref.at[slot], arrived.at[slot]
        )

    for tap_row in range(slots):
        fetch(tap_row).start()
    channels = gain_ref.shape[-1]
    height, across = mine_ref.shape[:2]
    cells = height * across
    core = core_ref[0]

    parts = rim_theirs_ref[0:16, channels:].astype(F32)
    sums = sums_ref[...] + parts[0:2] + parts[2:4] + parts[4:6]
    sums = jnp.concatenate([sums, jnp.zeros((6, LANES), F32)], axis=0)
    spread = dot(sums, group_matrix(channels, True), precision=lax.Precision.HIGHEST)
    average = spread[0:1] / members
    mean_square = spread[1:2] / members
    scale = lax.rsqrt(mean_square - average * average + 1e-05) * gain_ref[...]
    offset = shift_ref[...] - average * scale
    size = 256
    matrix = shuffle_matrix(64)
    for side, ref in enumerate((mine_ref, theirs_ref)):
        for k in range(0, channels, size):
            lanes = slice(k, k + size)
            value = ref[:, :, lanes].reshape(cells, size).astype(F32)
            value = value * scale[:, lanes] + offset[:, lanes]
            value = (0.5 * value) * (1.0 + jnp.tanh(0.5 * value))
            act_ref[side, :, lanes] = dot(value.astype(BF), matrix)
    for side, ref in enumerate((rim_mine_ref, rim_theirs_ref)):
        for k in range(0, channels, size):
            lanes = slice(k, k + size)
            rim_ref[side, :, lanes] = dot(ref[:, lanes], matrix)

    column = iota((across, channels), 0)

    def spread_row(side, line, value, left, right):
        before = jnp.where(column == 0, left, pltpu.roll(value, 1, 0))
        after = jnp.where(column == across - 1, right, pltpu.roll(value, across - 1, 0))
        for at, shifted in enumerate((before, value, after)):
            padded_ref[side, line, :, at * channels : (at + 1) * channels] = shifted.astype(BF)

    for side in range(2):
        other = 1 - side
        is_left = core == side
        for line, base in ((0, 0), (height + 1, 2 * across)):
            corner = across + (height - 1 if line == 0 else 0)
            far = rim_ref[side, base + corner : base + corner + 1]
            next_last = rim_ref[other, base + across - 1 : base + across]
            next_first = rim_ref[other, base : base + 1]
            value = rim_ref[side, base : base + across]
            spread_row(
                side, line, value, jnp.where(is_left, far, next_last), jnp.where(is_left, next_first, far)
            )
        outer_at = 4 * across
        inner_at = 4 * across + height

        @pl.loop(0, height, unroll=4)
        def _(r):
            outer = rim_ref[side, pl.ds(outer_at + r, 1)]
            inner = rim_ref[other, pl.ds(inner_at + r, 1)]
            value = act_ref[side, pl.ds(pl.multiple_of(r * across, across), across)]
            spread_row(
                side, r + 1, value, jnp.where(is_left, outer, inner), jnp.where(is_left, inner, outer)
            )

    half = channels // 2

    def row_product(tap_row):
        fetch(tap_row).wait()
        source = padded_ref[:, tap_row : tap_row + height].reshape(2 * cells, 3 * channels)
        return dot(source, held_ref[tap_row % slots].reshape(3 * channels, half))

    total_ref[...] = row_product(0)
    fetch(2).start()
    total_ref[...] += row_product(1)
    last = row_product(2)
    extra = bias_ref[...] + time_ref[0:1]
    extra = jnp.where(core == 0, extra[:, :half], extra[:, half:])
    for side, ref in enumerate((mine_ref, theirs_ref)):
        image = jnp.where(core == 0, ref[:, :, :half], ref[:, :, half:]).reshape(cells, half).astype(F32)
        rows = slice(side * cells, (side + 1) * cells)
        out_ref[rows] = (image + (total_ref[rows] + last[rows] + extra)).astype(BF)


def convolve(core, sums, mine, theirs, rim_mine, rim_theirs, gain, shift, bias, time_shift, weights, members):
    height, across, channels = mine.shape
    cells = height * across
    half = channels // 2
    whole = pl.BlockSpec(memory_space=pltpu.VMEM)
    small = pl.BlockSpec(memory_space=pltpu.SMEM)
    rim_rows = rim_mine.shape[0]
    return pl.pallas_call(
        functools.partial(conv_kernel, members=members),
        in_specs=[small] + [whole] * 9 + [pl.BlockSpec(memory_space=pl.ANY)],
        out_specs=whole,
        out_shape=jax.ShapeDtypeStruct((2 * cells, half), BF),
        scratch_shapes=[
            pltpu.VMEM((2, cells, channels), F32),
            pltpu.VMEM((2, rim_rows, channels), F32),
            pltpu.VMEM((2, height + 2, across, 3 * channels), BF),
            pltpu.VMEM((2 * cells, half), F32),
            pltpu.VMEM((2, 3, channels, half), BF),
            pltpu.SemaphoreType.DMA((2,)),
        ],
        compiler_params=params(32),
        cost_estimate=pl.CostEstimate(
            flops=36 * cells * channels * half, bytes_accessed=18 * channels * half, transcendentals=2 * cells * channels
        ),
    )(core, sums, mine, theirs, rim_mine, rim_theirs, gain, shift, bias, time_shift, from_hbm(weights))


def stale_kernel(near_ref, far_ref, key_ref, value_ref, keys_ref, values_ref):
    pooled = jnp.concatenate([near_ref[...], far_ref[...]], axis=0)
    keys_ref[...] = dot(pooled, key_ref[...]).astype(BF)
    values_ref[...] = dot(pooled, value_ref[...]).astype(BF)


def stale_pass(near, far, key_weight, value_weight):
    rows, channels = near.shape
    half = key_weight.shape[1]
    whole = pl.BlockSpec(memory_space=pltpu.VMEM)
    return pl.pallas_call(
        stale_kernel,
        in_specs=[whole] * 4,
        out_specs=[whole] * 2,
        out_shape=[jax.ShapeDtypeStruct((2 * rows, half), BF)] * 2,
        compiler_params=params(16),
        cost_estimate=pl.CostEstimate(
            flops=8 * rows * channels * half, bytes_accessed=4 * channels * half, transcendentals=0
        ),
    )(near, far, key_weight, value_weight)


def attention_kernel(
    core_ref, mine_ref, theirs_ref, gain_ref, query_ref, key_ref, value_ref, near_keys_ref, near_values_ref,
    beyond_ref, far_ref, out_weight_ref, send_ref, keep_ref, normed_ref, q_ref, k_ref, v_ref, mixed_ref, stale_keys_ref, stale_values_ref,
):
    rows, half = mine_ref.shape
    cells = rows // 2
    channels = 2 * half
    first = core_ref[0] == 0
    matrix = shuffle_matrix(64)
    for side in range(2):
        own = mine_ref[side * cells : (side + 1) * cells].astype(F32)
        other = theirs_ref[(1 - side) * cells : (2 - side) * cells].astype(F32)
        low = jnp.where(first, own, other)
        high = jnp.where(first, other, own)
        residual = jnp.concatenate([low, high], axis=1)
        if side == 0:
            keep_ref[...] = residual
        average = jnp.sum(residual, axis=1, keepdims=True) / channels
        centred = residual - average
        deviation = jnp.sum(centred * centred, axis=1, keepdims=True) / channels
        normed = (centred * lax.rsqrt(deviation + 1e-05) * gain_ref[...]).astype(BF)
        for k in range(0, channels, 256):
            normed_ref[side * cells : (side + 1) * cells, k : k + 256] = dot(
                normed[:, k : k + 256], matrix
            ).astype(BF)
    near_rows = near_keys_ref.shape[0]
    stale_keys_ref[:near_rows] = near_keys_ref[...]
    stale_values_ref[:near_rows] = near_values_ref[...]
    pooled = jnp.concatenate([beyond_ref[...], far_ref[...]], axis=0)
    stale_keys_ref[near_rows:] = dot(pooled, key_ref[...]).astype(BF)
    stale_values_ref[near_rows:] = dot(pooled, value_ref[...]).astype(BF)
    normed = normed_ref[...]
    q_ref[...] = (dot(normed, query_ref[...]).astype(BF) * BF(1.0 / math.sqrt(HEAD_DIM))).astype(BF)
    k_ref[...] = dot(normed, key_ref[...]).astype(BF)
    v_ref[...] = dot(normed, value_ref[...]).astype(BF)

    ones = jnp.ones((cells, LANES), BF)
    stale_ones = jnp.ones((stale_keys_ref.shape[0], LANES), BF)
    lane = iota((cells, LANES), 1)
    for side in range(2):
        at = slice(side * cells, (side + 1) * cells)
        for pair in range(half // LANES):
            lanes = slice(pair * LANES, (pair + 1) * LANES)
            q = q_ref[at, lanes]
            zero = jnp.zeros_like(q)
            stacked = jnp.concatenate(
                [jnp.where(lane < HEAD_DIM, q, zero), jnp.where(lane < HEAD_DIM, zero, q)], axis=0
            )
            fresh = dot_t(stacked, k_ref[at, lanes])
            stale = dot_t(stacked, stale_keys_ref[:, lanes])
            highest = jnp.maximum(
                jnp.max(fresh, axis=1, keepdims=True), jnp.max(stale, axis=1, keepdims=True)
            )
            fresh = jnp.exp(fresh - highest).astype(BF)
            stale = jnp.exp(stale - highest).astype(BF)
            mixed = dot(fresh, jnp.concatenate([v_ref[at, lanes], ones], axis=1))
            mixed += dot(stale, jnp.concatenate([stale_values_ref[:, lanes], stale_ones], axis=1))
            mixed = mixed[:, :LANES] / mixed[:, LANES:]
            mixed_ref[at, lanes] = jnp.where(lane < HEAD_DIM, mixed[:cells], mixed[cells:]).astype(BF)
    mixture = shuffle(mixed_ref[...], 32).astype(BF)
    send_ref[...] = dot(mixture[cells:], out_weight_ref[...]).astype(BF)
    keep_ref[...] += dot(mixture[:cells], out_weight_ref[...])


def attention_pass(core, mine, theirs, gain, query, key, value, near_keys, near_values, beyond, far, out_weight):
    rows, half = mine.shape
    channels = 2 * half
    cells = rows // 2
    whole = pl.BlockSpec(memory_space=pltpu.VMEM)
    small = pl.BlockSpec(memory_space=pltpu.SMEM)
    return pl.pallas_call(
        attention_kernel,
        in_specs=[small] + [whole] * 11,
        out_specs=[whole] * 2,
        out_shape=[
            jax.ShapeDtypeStruct((cells, channels), BF),
            jax.ShapeDtypeStruct((cells, channels), F32),
        ],
        scratch_shapes=[
            pltpu.VMEM((rows, channels), BF),
            pltpu.VMEM((rows, half), BF),
            pltpu.VMEM((rows, half), BF),
            pltpu.VMEM((rows, half), BF),
            pltpu.VMEM((rows, half), BF),
            pltpu.VMEM((4 * far.shape[0], half), BF),
            pltpu.VMEM((4 * far.shape[0], half), BF),
        ],
        compiler_params=params(28),
    )(core, mine, theirs, gain, query, key, value, near_keys, near_values, beyond, far, out_weight)


def swap(values, axis, step):
    count = lax.axis_size(axis)
    return lax.ppermute(values, axis, [(i, i ^ step) for i in range(count)])


def steps_over(axis, first):
    count = lax.axis_size(axis)
    return [(axis, 2 * m - 1) for m in (1 << k for k in range(count.bit_length() - 1)) if m >= first]


def split_sums(sums):
    high = lax.reduce_precision(sums, 8, 7)
    rest = sums - high
    middle = lax.reduce_precision(rest, 8, 7)
    low = rest - middle
    parts = jnp.concatenate([high, middle, low, jnp.zeros((10, LANES), F32)])
    return parts.astype(BF)


def join_sums(parts):
    parts = parts.astype(F32)
    return parts[0:2] + parts[2:4] + parts[4:6]


def tie(first, second):
    return lax.optimization_barrier((first, second))


def on_device(
    image,
    stale_first,
    stale_normed,
    timestep,
    time_weight,
    gain_first,
    shift_first,
    codes_first,
    table_first,
    bias_first,
    attn_gain,
    query_codes,
    query_table,
    key_codes,
    key_table,
    value_codes,
    value_table,
    out_codes,
    out_table,
):
    height, across, channels = image.shape
    cells = height * across
    rows = lax.axis_size("row")
    cols = lax.axis_size("col")
    members = cells * rows * cols * (channels // GROUPS)
    core = (lax.axis_index("col") % 2).astype(jnp.int32)[None]

    sums, edges, pooled, time_shift = first_pass(core, timestep, image, stale_first, stale_normed, time_weight)

    row_at = lax.axis_index("row")
    col_at = lax.axis_index("col")
    beside = jnp.where(core[0] == 0, col_at - 1, col_at + 1)
    hops = steps_over("col", 2) + steps_over("row", 1)
    chunks = [(0, 2), (2, 6), (6, 9)]
    outer = jnp.zeros_like(edges[0])
    above = below = jnp.zeros((height + across, channels), BF)
    near = pooled
    weights = None
    token = sums
    for at, (axis, step) in enumerate(hops):
        last = at == len(hops) - 1
        (sums, near), token = tie((sums, near), token)
        if axis == "col":
            border = edges[0]
        else:
            partner = row_at ^ step
            border = jnp.concatenate([jnp.where(partner > row_at, edges[3], edges[2]), outer])
        parts = jnp.pad(split_sums(sums), ((0, border.shape[0] - across), (0, 0)))
        border = jnp.concatenate([border, parts], axis=1)
        if last:
            got_border = swap(border, axis, step)
            final = (near, axis, step)
            far_near = swap(near, "col", 1)
        else:
            payload = jnp.concatenate([border, jnp.pad(near, ((0, 0), (0, LANES)))])
            got = swap(payload, axis, step)
            got_border = got[: border.shape[0]]
        if at == 1:
            partner_image = swap(image, "col", 1)
        if at < len(chunks):
            weights, token = decode_taps(core, token, codes_first, table_first, weights, *chunks[at])
        elif at == len(chunks):
            query, key, value, token = decode_matrices(
                core, token, (query_codes, key_codes, value_codes), (query_table, key_table, value_table), False
            )
        sums = sums + join_sums(got_border[:across, channels:])
        cells_got = got_border[:, :channels]
        if axis == "col":
            outer = jnp.where((col_at ^ step) == beside, cells_got, outer)
        else:
            above = jnp.where(partner == row_at - 1, cells_got, above)
            below = jnp.where(partner == row_at + 1, cells_got, below)
        if not last:
            near = jnp.concatenate([near, got[border.shape[0] :, :channels]])
    (above, below, sums), token = tie((above, below, sums), token)
    rim = jnp.concatenate([above, below, outer, edges[1]])
    parts = jnp.pad(split_sums(sums), ((0, rim.shape[0] - across), (0, 0)))
    partner_rim = swap(jnp.concatenate([rim, parts], axis=1), "col", 1)
    beyond = swap(*final)
    near_keys, near_values = stale_pass(near, far_near, key, value)
    sums, near_keys = tie(sums, near_keys)

    residual = convolve(
        core, sums, image, partner_image, rim, partner_rim, gain_first[None], shift_first[None],
        bias_first[None], time_shift, weights, members,
    )
    (residual, beyond), token = tie((residual, beyond), token)
    partner_residual = swap(residual, "col", 1)
    far = swap(beyond, "col", 1)
    out_weight, _ = decode_matrices(core, token, (out_codes,), (out_table,), True)
    send, keep = attention_pass(
        core, residual, partner_residual, attn_gain[None], query, key, value, near_keys, near_values, beyond, far, out_weight
    )
    output = keep + swap(send, "col", 1).astype(F32)
    return output.astype(BF).reshape(height, across, channels)


def solution(mesh):
    split = P("row", "col", None)
    in_specs = (split,) * 3 + (P(),) * 16
    return jax.shard_map(on_device, mesh=mesh, in_specs=in_specs, out_specs=split, check_vma=False)
```

```python
import functools
import math

import jax
import jax.numpy as jnp
from jax import lax
from jax.experimental import pallas as pl
from jax.experimental.pallas import tpu as pltpu
from jax.sharding import PartitionSpec as P

HEAD_DIM = 64
GROUPS = 32
TEMB = 320
POOL = 4
LANES = 128
BF = jnp.bfloat16
F32 = jnp.float32


def params(mebibytes):
    return pltpu.CompilerParams(vmem_limit_bytes=mebibytes * 2**20)


def dot(a, b, **extra):
    return jnp.dot(a, b, preferred_element_type=F32, **extra)


def dot_t(a, b):
    return lax.dot_general(a, b, (((1,), (1,)), ((), ())), preferred_element_type=F32)


def from_hbm(values):
    return pltpu.with_memory_space_constraint(values, pltpu.HBM)


def whole_block(shape):
    return pl.BlockSpec(shape, lambda *at: (0,) * len(shape))


def iota(shape, dim):
    return lax.broadcasted_iota(jnp.int32, shape, dim)


def shuffle_matrix(words):
    size = 4 * words
    row = iota((size, size), 0)
    col = iota((size, size), 1)
    return (row == 4 * (col % words) + col // words).astype(F32).astype(BF)


def shuffle(values, words):
    size = 4 * words
    matrix = shuffle_matrix(words)
    return jnp.concatenate(
        [dot(values[:, k : k + size], matrix) for k in range(0, values.shape[1], size)], axis=1
    )


def group_matrix(channels, transposed):
    members = channels // GROUPS
    shape = (LANES, channels) if transposed else (channels, LANES)
    channel = iota(shape, 1 if transposed else 0)
    group = iota(shape, 0 if transposed else 1)
    return ((channel >= group * members) & (channel < (group + 1) * members)).astype(F32)


def first_kernel(core_ref, step_ref, image_ref, first_ref, normed_ref, time_ref, sums_ref, edge_ref, pool_ref, shift_ref):
    channels = image_ref.shape[-1]
    height, across = first_ref.shape[:2]
    cells = height * across
    core = core_ref[0]
    image = image_ref[...].reshape(cells, channels).astype(F32)
    sums = jnp.sum(image, axis=0, keepdims=True)
    squares = jnp.sum(image * image, axis=0, keepdims=True)
    row8 = iota((8, channels), 0)
    both = jnp.where(row8 == 0, sums, jnp.where(row8 == 1, squares, 0.0))
    sums_ref[...] = dot(both, group_matrix(channels, False), precision=lax.Precision.HIGHEST)[0:2]

    cells_first = first_ref[...].reshape(cells, channels)
    row = iota((height, cells), 0)
    cell = iota((height, cells), 1)
    outer = jnp.where(core == 0, 0, across - 1)
    pick_outer = (cell == row * across + outer).astype(F32).astype(BF)
    pick_inner = (cell == row * across + (across - 1 - outer)).astype(F32).astype(BF)
    edge_ref[0] = dot(pick_outer, cells_first).astype(BF)
    edge_ref[1] = dot(pick_inner, cells_first).astype(BF)
    edge_ref[2] = first_ref[0]
    edge_ref[3] = first_ref[height - 1]

    pools = pool_ref.shape[0]
    pool = iota((pools, cells), 0)
    cell = iota((pools, cells), 1)
    in_row = cell // across // POOL == pool // (across // POOL)
    in_col = cell % across // POOL == pool % (across // POOL)
    average = jnp.where(in_row & in_col, 1.0 / (POOL * POOL), 0.0).astype(BF)
    pooled = dot(average, normed_ref[...].reshape(cells, channels)).astype(BF)
    pool_ref[...] = shuffle(pooled, 64).astype(BF)

    half = TEMB // 2
    place = iota((8, TEMB), 1)
    index = jnp.where(place < half, place, place - half).astype(F32)
    frequency = jnp.exp(-math.log(10000.0) * index / half)
    angle = step_ref[0].astype(F32) * frequency
    sinusoid = jnp.where(place < half, jnp.cos(angle), jnp.sin(angle)).astype(BF)
    shift = dot(sinusoid, time_ref[...])
    shift_ref[...] = shift * jax.nn.sigmoid(shift)


def first_pass(core, timestep, image, stale_first, stale_normed, time_weight):
    height, across, channels = image.shape
    pools = (height // POOL) * (across // POOL)
    small = pl.BlockSpec(memory_space=pltpu.SMEM)
    big = [from_hbm(x) for x in (image, stale_first, stale_normed, time_weight)]
    shapes = [(2, LANES), (4, height, channels), (pools, channels), (8, channels)]
    return pl.pallas_call(
        first_kernel,
        grid=(1,),
        in_specs=[small, small] + [whole_block(x.shape) for x in (image, stale_first, stale_normed, time_weight)],
        out_specs=[whole_block(shape) for shape in shapes],
        out_shape=[jax.ShapeDtypeStruct(shape, kind) for shape, kind in zip(shapes, (F32, BF, BF, F32))],
        compiler_params=params(16),
    )(core, timestep, *big)


def decode_tile(words, words16, low, high, place):
    lows = []
    highs = []
    for k in range(0, words.shape[0], 8):
        index = words[k : k + 8]
        if place:
            index = index >> (4 * place)
        index = index & 7
        lows.append(jnp.take_along_axis(low, index, axis=0, mode="promise_in_bounds"))
        highs.append(jnp.take_along_axis(high, index, axis=0, mode="promise_in_bounds"))
    bit = 4 * place + 3
    upper = (words16 & jnp.int16(1 << bit if bit < 15 else -(1 << 15))) != 0
    return jnp.where(
        upper, jnp.concatenate(highs, axis=0).astype(BF), jnp.concatenate(lows, axis=0).astype(BF)
    )


def decode_lanes(codes_ref, low, high, weight_ref, block):
    for g in range(codes_ref.shape[0] // block):
        words = codes_ref[g * block : (g + 1) * block]
        words16 = words.astype(jnp.int16)
        for place in range(4):
            at = (4 * g + place) * block
            weight_ref[at : at + block] = decode_tile(words, words16, low, high, place)


def lanes_at(index):
    return pl.ds(index * LANES, LANES)


def decode_cost(weights):
    return pl.CostEstimate(flops=8 * weights, bytes_accessed=3 * weights, transcendentals=0)


def taps_kernel(core_ref, token_ref, table_ref, codes_ref, *refs, start, count):
    weight_ref, token_out_ref, words_ref, held_ref, came, went = refs[-6:]
    slots = words_ref.shape[0]
    blocks = words_ref.shape[2] // LANES
    first = core_ref[0] * blocks
    token_out_ref[...] = token_ref[...]

    def far_lanes(block):
        return pl.ds(pl.multiple_of((first + block) * LANES, LANES), LANES)

    def fetch(tap, block):
        slot = tap % slots
        return pltpu.make_async_copy(
            codes_ref.at[start + tap, :, far_lanes(block)],
            words_ref.at[slot, :, lanes_at(block)],
            came.at[slot, block],
        )

    def store(tap, block):
        slot = tap % 2
        return pltpu.make_async_copy(
            held_ref.at[slot, :, lanes_at(block)],
            weight_ref.at[start + tap, :, lanes_at(block)],
            went.at[slot, block],
        )

    for tap in range(min(slots, count)):
        for block in range(blocks):
            fetch(tap, block).start()

    @pl.loop(0, count)
    def _(tap):
        for block in range(blocks):
            fetch(tap, block).wait()

            @pl.when(tap >= 2)
            def _():
                store(tap - 2, block).wait()

            decode_lanes(
                words_ref.at[tap % slots, :, lanes_at(block)],
                table_ref[0:8, far_lanes(block)],
                table_ref[8:16, far_lanes(block)],
                held_ref.at[tap % 2, :, lanes_at(block)],
                64,
            )
            store(tap, block).start()

            @pl.when(tap + slots < count)
            def _():
                fetch(tap + slots, block).start()

    for tap in range(max(count - 2, 0), count):
        for block in range(blocks):
            store(tap, block).wait()


def decode_taps(core, token, codes, table, weights, start, stop):
    words, channels = codes.shape[1:]
    half = channels // 2
    count = stop - start
    into = [] if weights is None else [from_hbm(weights)]
    whole = pl.BlockSpec(memory_space=pltpu.VMEM)
    far = pl.BlockSpec(memory_space=pl.ANY)
    return pl.pallas_call(
        functools.partial(taps_kernel, start=start, count=count),
        in_specs=[pl.BlockSpec(memory_space=pltpu.SMEM), whole, whole, far] + [far] * len(into),
        out_specs=[far, whole],
        out_shape=[
            pltpu.HBM((codes.shape[0], 4 * words, half), BF),
            jax.ShapeDtypeStruct(token.shape, token.dtype),
        ],
        scratch_shapes=[
            pltpu.VMEM((3, words, half), jnp.int32),
            pltpu.VMEM((2, 4 * words, half), BF),
            pltpu.SemaphoreType.DMA((3, half // LANES)),
            pltpu.SemaphoreType.DMA((2, half // LANES)),
        ],
        input_output_aliases={4: 0} if into else {},
        compiler_params=params(10),
        cost_estimate=decode_cost(count * 4 * words * half),
    )(core, token, table, from_hbm(codes), *into)


def matrices_kernel(core_ref, token_ref, *refs, count, by_rows, block):
    tables = refs[:count]
    codes = refs[count : 2 * count]
    weights = refs[2 * count : 3 * count]
    token_out_ref, words_ref, came = refs[3 * count :]
    token_out_ref[...] = token_ref[...]
    rows = words_ref.shape[1]
    blocks = words_ref.shape[2] // LANES
    core = core_ref[0]
    first = 0 if by_rows else core * blocks
    row = pl.multiple_of(core * rows, 8) if by_rows else 0

    def far_lanes(at):
        return lanes_at(at) if by_rows else pl.ds(pl.multiple_of((first + at) * LANES, LANES), LANES)

    def fetch(k, at):
        return pltpu.make_async_copy(
            codes[k].at[pl.ds(row, rows), far_lanes(at)], words_ref.at[k, :, lanes_at(at)], came.at[k, at]
        )

    for k in range(count):
        for at in range(blocks):
            fetch(k, at).start()
    for k in range(count):
        for at in range(blocks):
            fetch(k, at).wait()
            decode_lanes(
                words_ref.at[k, :, lanes_at(at)],
                tables[k][0:8, far_lanes(at)],
                tables[k][8:16, far_lanes(at)],
                weights[k].at[:, lanes_at(at)],
                block,
            )


def decode_matrices(core, token, codes, tables, by_rows):
    count = len(codes)
    words, channels = codes[0].shape
    rows, columns = (words // 2, channels) if by_rows else (words, channels // 2)
    whole = pl.BlockSpec(memory_space=pltpu.VMEM)
    return pl.pallas_call(
        functools.partial(matrices_kernel, count=count, by_rows=by_rows, block=32 if by_rows else 64),
        in_specs=[pl.BlockSpec(memory_space=pltpu.SMEM)]
        + [whole] * (1 + count)
        + [pl.BlockSpec(memory_space=pl.ANY)] * count,
        out_specs=[whole] * (count + 1),
        out_shape=[jax.ShapeDtypeStruct((4 * rows, columns), BF)] * count
        + [jax.ShapeDtypeStruct(token.shape, token.dtype)],
        scratch_shapes=[
            pltpu.VMEM((count, rows, columns), jnp.int32),
            pltpu.SemaphoreType.DMA((count, columns // LANES)),
        ],
        compiler_params=params(10),
        cost_estimate=decode_cost(count * 4 * rows * columns),
    )(core, token, *tables, *[from_hbm(x) for x in codes])


def conv_kernel(
    core_ref, sums_ref, mine_ref, theirs_ref, rim_mine_ref, rim_theirs_ref, gain_ref, shift_ref, bias_ref, time_ref,
    weight_ref, out_ref, act_ref, rim_ref, padded_ref, total_ref, held_ref, arrived, *, members,
):
    slots = held_ref.shape[0]

    def fetch(tap_row):
        slot = tap_row % slots
        return pltpu.make_async_copy(
            weight_ref.at[3 * tap_row : 3 * tap_row + 3], held_ref.at[slot], arrived.at[slot]
        )

    for tap_row in range(slots):
        fetch(tap_row).start()
    channels = gain_ref.shape[-1]
    height, across = mine_ref.shape[:2]
    cells = height * across
    core = core_ref[0]

    parts = rim_theirs_ref[0:16, channels:].astype(F32)
    sums = sums_ref[...] + parts[0:2] + parts[2:4] + parts[4:6]
    sums = jnp.concatenate([sums, jnp.zeros((6, LANES), F32)], axis=0)
    spread = dot(sums, group_matrix(channels, True), precision=lax.Precision.HIGHEST)
    average = spread[0:1] / members
    mean_square = spread[1:2] / members
    scale = lax.rsqrt(mean_square - average * average + 1e-05) * gain_ref[...]
    offset = 0.5 * (shift_ref[...] - average * scale)
    scale = 0.5 * scale
    size = 256
    matrix = shuffle_matrix(64)
    for side, ref in enumerate((mine_ref, theirs_ref)):
        for k in range(0, channels, size):
            lanes = slice(k, k + size)
            value = ref[:, :, lanes].reshape(cells, size).astype(F32)
            value = value * scale[:, lanes] + offset[:, lanes]
            value = value + value * jnp.tanh(value)
            act_ref[side, :, lanes] = dot(value.astype(BF), matrix)
    for side, ref in enumerate((rim_mine_ref, rim_theirs_ref)):
        for k in range(0, channels, size):
            lanes = slice(k, k + size)
            rim_ref[side, :, lanes] = dot(ref[:, lanes], matrix)

    column = iota((across, channels), 0)

    def spread_row(side, line, value, left, right):
        before = jnp.where(column == 0, left, pltpu.roll(value, 1, 0))
        after = jnp.where(column == across - 1, right, pltpu.roll(value, across - 1, 0))
        for at, shifted in enumerate((before, value, after)):
            padded_ref[side, line, :, at * channels : (at + 1) * channels] = shifted.astype(BF)

    for side in range(2):
        other = 1 - side
        is_left = core == side
        for line, base in ((0, 0), (height + 1, 2 * across)):
            corner = across + (height - 1 if line == 0 else 0)
            far = rim_ref[side, base + corner : base + corner + 1]
            next_last = rim_ref[other, base + across - 1 : base + across]
            next_first = rim_ref[other, base : base + 1]
            value = rim_ref[side, base : base + across]
            spread_row(
                side, line, value, jnp.where(is_left, far, next_last), jnp.where(is_left, next_first, far)
            )
        outer_at = 4 * across
        inner_at = 4 * across + height

        @pl.loop(0, height, unroll=height)
        def _(r):
            outer = rim_ref[side, pl.ds(outer_at + r, 1)]
            inner = rim_ref[other, pl.ds(inner_at + r, 1)]
            value = act_ref[side, pl.ds(pl.multiple_of(r * across, across), across)]
            spread_row(
                side, r + 1, value, jnp.where(is_left, outer, inner), jnp.where(is_left, inner, outer)
            )

    half = channels // 2

    def row_product(tap_row):
        fetch(tap_row).wait()
        source = padded_ref[:, tap_row : tap_row + height].reshape(2 * cells, 3 * channels)
        return dot(source, held_ref[tap_row % slots].reshape(3 * channels, half))

    total_ref[...] = row_product(0)
    fetch(2).start()
    total_ref[...] += row_product(1)
    last = row_product(2)
    extra = bias_ref[...] + time_ref[0:1]
    extra = jnp.where(core == 0, extra[:, :half], extra[:, half:])
    for side, ref in enumerate((mine_ref, theirs_ref)):
        image = jnp.where(core == 0, ref[:, :, :half], ref[:, :, half:]).reshape(cells, half).astype(F32)
        rows = slice(side * cells, (side + 1) * cells)
        out_ref[rows] = (image + (total_ref[rows] + last[rows] + extra)).astype(BF)


def convolve(core, sums, mine, theirs, rim_mine, rim_theirs, gain, shift, bias, time_shift, weights, members):
    height, across, channels = mine.shape
    cells = height * across
    half = channels // 2
    whole = pl.BlockSpec(memory_space=pltpu.VMEM)
    small = pl.BlockSpec(memory_space=pltpu.SMEM)
    rim_rows = rim_mine.shape[0]
    return pl.pallas_call(
        functools.partial(conv_kernel, members=members),
        in_specs=[small] + [whole] * 9 + [pl.BlockSpec(memory_space=pl.ANY)],
        out_specs=whole,
        out_shape=jax.ShapeDtypeStruct((2 * cells, half), BF),
        scratch_shapes=[
            pltpu.VMEM((2, cells, channels), F32),
            pltpu.VMEM((2, rim_rows, channels), F32),
            pltpu.VMEM((2, height + 2, across, 3 * channels), BF),
            pltpu.VMEM((2 * cells, half), F32),
            pltpu.VMEM((2, 3, channels, half), BF),
            pltpu.SemaphoreType.DMA((2,)),
        ],
        compiler_params=params(32),
        cost_estimate=pl.CostEstimate(
            flops=36 * cells * channels * half, bytes_accessed=18 * channels * half, transcendentals=2 * cells * channels
        ),
    )(core, sums, mine, theirs, rim_mine, rim_theirs, gain, shift, bias, time_shift, from_hbm(weights))


def stale_kernel(near_ref, far_ref, key_ref, value_ref, keys_ref, values_ref):
    pooled = jnp.concatenate([near_ref[...], far_ref[...]], axis=0)
    keys_ref[...] = dot(pooled, key_ref[...]).astype(BF)
    values_ref[...] = dot(pooled, value_ref[...]).astype(BF)


def stale_pass(near, far, key_weight, value_weight):
    rows, channels = near.shape
    half = key_weight.shape[1]
    whole = pl.BlockSpec(memory_space=pltpu.VMEM)
    return pl.pallas_call(
        stale_kernel,
        in_specs=[whole] * 4,
        out_specs=[whole] * 2,
        out_shape=[jax.ShapeDtypeStruct((2 * rows, half), BF)] * 2,
        compiler_params=params(16),
        cost_estimate=pl.CostEstimate(
            flops=8 * rows * channels * half, bytes_accessed=4 * channels * half, transcendentals=0
        ),
    )(near, far, key_weight, value_weight)


def attention_kernel(
    core_ref, mine_ref, theirs_ref, gain_ref, query_ref, key_ref, value_ref, near_keys_ref, near_values_ref,
    beyond_ref, far_ref, out_weight_ref, send_ref, keep_ref, normed_ref, q_ref, k_ref, v_ref, mixed_ref, stale_keys_ref, stale_values_ref,
):
    rows, half = mine_ref.shape
    cells = rows // 2
    channels = 2 * half
    first = core_ref[0] == 0
    matrix = shuffle_matrix(64)
    for side in range(2):
        own = mine_ref[side * cells : (side + 1) * cells].astype(F32)
        other = theirs_ref[(1 - side) * cells : (2 - side) * cells].astype(F32)
        low = jnp.where(first, own, other)
        high = jnp.where(first, other, own)
        residual = jnp.concatenate([low, high], axis=1)
        if side == 0:
            keep_ref[...] = residual
        average = jnp.sum(residual, axis=1, keepdims=True) / channels
        centred = residual - average
        deviation = jnp.sum(centred * centred, axis=1, keepdims=True) / channels
        normed = (centred * lax.rsqrt(deviation + 1e-05) * gain_ref[...]).astype(BF)
        for k in range(0, channels, 256):
            normed_ref[side * cells : (side + 1) * cells, k : k + 256] = dot(
                normed[:, k : k + 256], matrix
            ).astype(BF)
    near_rows = near_keys_ref.shape[0]
    stale_keys_ref[:near_rows] = near_keys_ref[...]
    stale_values_ref[:near_rows] = near_values_ref[...]
    pooled = jnp.concatenate([beyond_ref[...], far_ref[...]], axis=0)
    stale_keys_ref[near_rows:] = dot(pooled, key_ref[...]).astype(BF)
    stale_values_ref[near_rows:] = dot(pooled, value_ref[...]).astype(BF)
    normed = normed_ref[...]
    q_ref[...] = (dot(normed, query_ref[...]).astype(BF) * BF(1.0 / math.sqrt(HEAD_DIM))).astype(BF)
    k_ref[...] = dot(normed, key_ref[...]).astype(BF)
    v_ref[...] = dot(normed, value_ref[...]).astype(BF)

    ones = jnp.ones((cells, LANES), BF)
    stale_ones = jnp.ones((stale_keys_ref.shape[0], LANES), BF)
    lane = iota((cells, LANES), 1)
    for side in range(2):
        at = slice(side * cells, (side + 1) * cells)
        for pair in range(half // LANES):
            lanes = slice(pair * LANES, (pair + 1) * LANES)
            q = q_ref[at, lanes]
            zero = jnp.zeros_like(q)
            stacked = jnp.concatenate(
                [jnp.where(lane < HEAD_DIM, q, zero), jnp.where(lane < HEAD_DIM, zero, q)], axis=0
            )
            fresh = dot_t(stacked, k_ref[at, lanes])
            stale = dot_t(stacked, stale_keys_ref[:, lanes])
            blocks = [x[:, k : k + LANES] for x in (fresh, stale) for k in range(0, x.shape[1], LANES)]
            highest = jnp.max(functools.reduce(jnp.maximum, blocks), axis=1, keepdims=True)
            fresh = jnp.exp(fresh - highest).astype(BF)
            stale = jnp.exp(stale - highest).astype(BF)
            mixed = dot(fresh, jnp.concatenate([v_ref[at, lanes], ones], axis=1))
            mixed += dot(stale, jnp.concatenate([stale_values_ref[:, lanes], stale_ones], axis=1))
            merged = jnp.where(lane < HEAD_DIM, mixed[:cells, :LANES], mixed[cells:, :LANES])
            weight = jnp.where(lane < HEAD_DIM, mixed[:cells, LANES:], mixed[cells:, LANES:])
            mixed_ref[at, lanes] = (merged / weight).astype(BF)
    mixture = shuffle(mixed_ref[...], 32).astype(BF)
    send_ref[...] = dot(mixture[cells:], out_weight_ref[...]).astype(BF)
    keep_ref[...] += dot(mixture[:cells], out_weight_ref[...])


def attention_pass(core, mine, theirs, gain, query, key, value, near_keys, near_values, beyond, far, out_weight):
    rows, half = mine.shape
    channels = 2 * half
    cells = rows // 2
    whole = pl.BlockSpec(memory_space=pltpu.VMEM)
    small = pl.BlockSpec(memory_space=pltpu.SMEM)
    return pl.pallas_call(
        attention_kernel,
        in_specs=[small] + [whole] * 11,
        out_specs=[whole] * 2,
        out_shape=[
            jax.ShapeDtypeStruct((cells, channels), BF),
            jax.ShapeDtypeStruct((cells, channels), F32),
        ],
        scratch_shapes=[
            pltpu.VMEM((rows, channels), BF),
            pltpu.VMEM((rows, half), BF),
            pltpu.VMEM((rows, half), BF),
            pltpu.VMEM((rows, half), BF),
            pltpu.VMEM((rows, half), BF),
            pltpu.VMEM((4 * far.shape[0], half), BF),
            pltpu.VMEM((4 * far.shape[0], half), BF),
        ],
        compiler_params=params(28),
    )(core, mine, theirs, gain, query, key, value, near_keys, near_values, beyond, far, out_weight)


def swap(values, axis, step):
    count = lax.axis_size(axis)
    return lax.ppermute(values, axis, [(i, i ^ step) for i in range(count)])


def steps_over(axis, first):
    count = lax.axis_size(axis)
    return [(axis, 2 * m - 1) for m in (1 << k for k in range(count.bit_length() - 1)) if m >= first]


def split_sums(sums):
    high = lax.reduce_precision(sums, 8, 7)
    rest = sums - high
    middle = lax.reduce_precision(rest, 8, 7)
    low = rest - middle
    parts = jnp.concatenate([high, middle, low, jnp.zeros((10, LANES), F32)])
    return parts.astype(BF)


def join_sums(parts):
    parts = parts.astype(F32)
    return parts[0:2] + parts[2:4] + parts[4:6]


def tie(first, second):
    return lax.optimization_barrier((first, second))


def on_device(
    image,
    stale_first,
    stale_normed,
    timestep,
    time_weight,
    gain_first,
    shift_first,
    codes_first,
    table_first,
    bias_first,
    attn_gain,
    query_codes,
    query_table,
    key_codes,
    key_table,
    value_codes,
    value_table,
    out_codes,
    out_table,
):
    height, across, channels = image.shape
    cells = height * across
    rows = lax.axis_size("row")
    cols = lax.axis_size("col")
    members = cells * rows * cols * (channels // GROUPS)
    core = (lax.axis_index("col") % 2).astype(jnp.int32)[None]

    sums, edges, pooled, time_shift = first_pass(core, timestep, image, stale_first, stale_normed, time_weight)

    row_at = lax.axis_index("row")
    col_at = lax.axis_index("col")
    beside = jnp.where(core[0] == 0, col_at - 1, col_at + 1)
    hops = steps_over("col", 2) + steps_over("row", 1)
    chunks = [(0, 2), (2, 6), (6, 9)]
    outer = jnp.zeros_like(edges[0])
    above = below = jnp.zeros((height + across, channels), BF)
    near = pooled
    weights = None
    token = sums
    for at, (axis, step) in enumerate(hops):
        last = at == len(hops) - 1
        (sums, near), token = tie((sums, near), token)
        if axis == "col":
            border = edges[0]
        else:
            partner = row_at ^ step
            border = jnp.concatenate([jnp.where(partner > row_at, edges[3], edges[2]), outer])
        parts = jnp.pad(split_sums(sums), ((0, border.shape[0] - across), (0, 0)))
        border = jnp.concatenate([border, parts], axis=1)
        if last:
            got_border = swap(border, axis, step)
            final = (near, axis, step)
            far_near = swap(near, "col", 1)
        else:
            payload = jnp.concatenate([border, jnp.pad(near, ((0, 0), (0, LANES)))])
            got = swap(payload, axis, step)
            got_border = got[: border.shape[0]]
        if at == 1:
            partner_image = swap(image, "col", 1)
        if at < len(chunks):
            weights, token = decode_taps(core, token, codes_first, table_first, weights, *chunks[at])
        elif at == len(chunks):
            query, key, value, token = decode_matrices(
                core, token, (query_codes, key_codes, value_codes), (query_table, key_table, value_table), False
            )
        sums = sums + join_sums(got_border[:across, channels:])
        cells_got = got_border[:, :channels]
        if axis == "col":
            outer = jnp.where((col_at ^ step) == beside, cells_got, outer)
        else:
            above = jnp.where(partner == row_at - 1, cells_got, above)
            below = jnp.where(partner == row_at + 1, cells_got, below)
        if not last:
            near = jnp.concatenate([near, got[border.shape[0] :, :channels]])
    (above, below, sums), token = tie((above, below, sums), token)
    rim = jnp.concatenate([above, below, outer, edges[1]])
    parts = jnp.pad(split_sums(sums), ((0, rim.shape[0] - across), (0, 0)))
    partner_rim = swap(jnp.concatenate([rim, parts], axis=1), "col", 1)
    beyond = swap(*final)
    near_keys, near_values = stale_pass(near, far_near, key, value)
    sums, near_keys = tie(sums, near_keys)

    residual = convolve(
        core, sums, image, partner_image, rim, partner_rim, gain_first[None], shift_first[None],
        bias_first[None], time_shift, weights, members,
    )
    (residual, beyond), token = tie((residual, beyond), token)
    partner_residual = swap(residual, "col", 1)
    far = swap(beyond, "col", 1)
    out_weight, _ = decode_matrices(core, token, (out_codes,), (out_table,), True)
    send, keep = attention_pass(
        core, residual, partner_residual, attn_gain[None], query, key, value, near_keys, near_values, beyond, far, out_weight
    )
    output = keep + swap(send, "col", 1).astype(F32)
    return output.astype(BF).reshape(height, across, channels)


def solution(mesh):
    split = P("row", "col", None)
    in_specs = (split,) * 3 + (P(),) * 16
    return jax.shard_map(on_device, mesh=mesh, in_specs=in_specs, out_specs=split, check_vma=False)
```

```python
import functools
import math

import jax
import jax.numpy as jnp
from jax import lax
from jax.experimental import pallas as pl
from jax.experimental.pallas import tpu as pltpu
from jax.sharding import PartitionSpec as P

HEAD_DIM = 64
GROUPS = 32
TEMB = 320
POOL = 4
LANES = 128
BF = jnp.bfloat16
F32 = jnp.float32


def params(mebibytes):
    return pltpu.CompilerParams(vmem_limit_bytes=mebibytes * 2**20)


def dot(a, b, **extra):
    return jnp.dot(a, b, preferred_element_type=F32, **extra)


def dot_t(a, b):
    return lax.dot_general(a, b, (((1,), (1,)), ((), ())), preferred_element_type=F32)


def from_hbm(values):
    return pltpu.with_memory_space_constraint(values, pltpu.HBM)


def whole_block(shape):
    return pl.BlockSpec(shape, lambda *at: (0,) * len(shape))


def iota(shape, dim):
    return lax.broadcasted_iota(jnp.int32, shape, dim)


def shuffle_matrix(words):
    size = 4 * words
    row = iota((size, size), 0)
    col = iota((size, size), 1)
    return (row == 4 * (col % words) + col // words).astype(F32).astype(BF)


def shuffle(values, words):
    size = 4 * words
    matrix = shuffle_matrix(words)
    return jnp.concatenate(
        [dot(values[:, k : k + size], matrix) for k in range(0, values.shape[1], size)], axis=1
    )


def group_matrix(channels, transposed):
    members = channels // GROUPS
    shape = (LANES, channels) if transposed else (channels, LANES)
    channel = iota(shape, 1 if transposed else 0)
    group = iota(shape, 0 if transposed else 1)
    return ((channel >= group * members) & (channel < (group + 1) * members)).astype(F32)


def first_kernel(core_ref, step_ref, image_ref, first_ref, normed_ref, time_ref, sums_ref, edge_ref, pool_ref, shift_ref):
    channels = image_ref.shape[-1]
    height, across = first_ref.shape[:2]
    cells = height * across
    core = core_ref[0]
    image = image_ref[...].reshape(cells, channels).astype(F32)
    sums = jnp.sum(image, axis=0, keepdims=True)
    squares = jnp.sum(image * image, axis=0, keepdims=True)
    row8 = iota((8, channels), 0)
    both = jnp.where(row8 == 0, sums, jnp.where(row8 == 1, squares, 0.0))
    sums_ref[...] = dot(both, group_matrix(channels, False), precision=lax.Precision.HIGHEST)[0:2]

    cells_first = first_ref[...].reshape(cells, channels)
    row = iota((height, cells), 0)
    cell = iota((height, cells), 1)
    outer = jnp.where(core == 0, 0, across - 1)
    pick_outer = (cell == row * across + outer).astype(F32).astype(BF)
    pick_inner = (cell == row * across + (across - 1 - outer)).astype(F32).astype(BF)
    edge_ref[0] = dot(pick_outer, cells_first).astype(BF)
    edge_ref[1] = dot(pick_inner, cells_first).astype(BF)
    edge_ref[2] = first_ref[0]
    edge_ref[3] = first_ref[height - 1]

    pools = pool_ref.shape[0]
    pool = iota((pools, cells), 0)
    cell = iota((pools, cells), 1)
    in_row = cell // across // POOL == pool // (across // POOL)
    in_col = cell % across // POOL == pool % (across // POOL)
    average = jnp.where(in_row & in_col, 1.0 / (POOL * POOL), 0.0).astype(BF)
    pooled = dot(average, normed_ref[...].reshape(cells, channels)).astype(BF)
    pool_ref[...] = shuffle(pooled, 64).astype(BF)

    half = TEMB // 2
    place = iota((8, TEMB), 1)
    index = jnp.where(place < half, place, place - half).astype(F32)
    frequency = jnp.exp(-math.log(10000.0) * index / half)
    angle = step_ref[0].astype(F32) * frequency
    sinusoid = jnp.where(place < half, jnp.cos(angle), jnp.sin(angle)).astype(BF)
    shift = dot(sinusoid, time_ref[...])
    shift_ref[...] = shift * jax.nn.sigmoid(shift)


def first_pass(core, timestep, image, stale_first, stale_normed, time_weight):
    height, across, channels = image.shape
    pools = (height // POOL) * (across // POOL)
    small = pl.BlockSpec(memory_space=pltpu.SMEM)
    big = [from_hbm(x) for x in (image, stale_first, stale_normed, time_weight)]
    shapes = [(2, LANES), (4, height, channels), (pools, channels), (8, channels)]
    return pl.pallas_call(
        first_kernel,
        grid=(1,),
        in_specs=[small, small] + [whole_block(x.shape) for x in (image, stale_first, stale_normed, time_weight)],
        out_specs=[whole_block(shape) for shape in shapes],
        out_shape=[jax.ShapeDtypeStruct(shape, kind) for shape, kind in zip(shapes, (F32, BF, BF, F32))],
        compiler_params=params(16),
    )(core, timestep, *big)


def decode_tile(words, words16, low, high, place):
    lows = []
    highs = []
    for k in range(0, words.shape[0], 8):
        index = words[k : k + 8]
        if place:
            index = index >> (4 * place)
        index = index & 7
        lows.append(jnp.take_along_axis(low, index, axis=0, mode="promise_in_bounds"))
        highs.append(jnp.take_along_axis(high, index, axis=0, mode="promise_in_bounds"))
    bit = 4 * place + 3
    upper = (words16 & jnp.int16(1 << bit if bit < 15 else -(1 << 15))) != 0
    return jnp.where(
        upper, jnp.concatenate(highs, axis=0).astype(BF), jnp.concatenate(lows, axis=0).astype(BF)
    )


def decode_lanes(codes_ref, low, high, weight_ref, block):
    for g in range(codes_ref.shape[0] // block):
        words = codes_ref[g * block : (g + 1) * block]
        words16 = words.astype(jnp.int16)
        for place in range(4):
            at = (4 * g + place) * block
            weight_ref[at : at + block] = decode_tile(words, words16, low, high, place)


def lanes_at(index):
    return pl.ds(index * LANES, LANES)


def decode_cost(weights):
    return pl.CostEstimate(flops=8 * weights, bytes_accessed=3 * weights, transcendentals=0)


def taps_kernel(core_ref, token_ref, table_ref, codes_ref, *refs, start, count):
    weight_ref, token_out_ref, words_ref, held_ref, came, went = refs[-6:]
    slots = words_ref.shape[0]
    blocks = words_ref.shape[2] // LANES
    first = core_ref[0] * blocks
    token_out_ref[...] = token_ref[...]

    def far_lanes(block):
        return pl.ds(pl.multiple_of((first + block) * LANES, LANES), LANES)

    def fetch(tap, block):
        slot = tap % slots
        return pltpu.make_async_copy(
            codes_ref.at[start + tap, :, far_lanes(block)],
            words_ref.at[slot, :, lanes_at(block)],
            came.at[slot, block],
        )

    def store(tap, block):
        slot = tap % 2
        return pltpu.make_async_copy(
            held_ref.at[slot, :, lanes_at(block)],
            weight_ref.at[start + tap, :, lanes_at(block)],
            went.at[slot, block],
        )

    for tap in range(min(slots, count)):
        for block in range(blocks):
            fetch(tap, block).start()

    @pl.loop(0, count)
    def _(tap):
        for block in range(blocks):
            fetch(tap, block).wait()

            @pl.when(tap >= 2)
            def _():
                store(tap - 2, block).wait()

            decode_lanes(
                words_ref.at[tap % slots, :, lanes_at(block)],
                table_ref[0:8, far_lanes(block)],
                table_ref[8:16, far_lanes(block)],
                held_ref.at[tap % 2, :, lanes_at(block)],
                64,
            )
            store(tap, block).start()

            @pl.when(tap + slots < count)
            def _():
                fetch(tap + slots, block).start()

    for tap in range(max(count - 2, 0), count):
        for block in range(blocks):
            store(tap, block).wait()


def decode_taps(core, token, codes, table, weights, start, stop):
    words, channels = codes.shape[1:]
    half = channels // 2
    count = stop - start
    into = [] if weights is None else [from_hbm(weights)]
    whole = pl.BlockSpec(memory_space=pltpu.VMEM)
    far = pl.BlockSpec(memory_space=pl.ANY)
    return pl.pallas_call(
        functools.partial(taps_kernel, start=start, count=count),
        in_specs=[pl.BlockSpec(memory_space=pltpu.SMEM), whole, whole, far] + [far] * len(into),
        out_specs=[far, whole],
        out_shape=[
            pltpu.HBM((codes.shape[0], 4 * words, half), BF),
            jax.ShapeDtypeStruct(token.shape, token.dtype),
        ],
        scratch_shapes=[
            pltpu.VMEM((3, words, half), jnp.int32),
            pltpu.VMEM((2, 4 * words, half), BF),
            pltpu.SemaphoreType.DMA((3, half // LANES)),
            pltpu.SemaphoreType.DMA((2, half // LANES)),
        ],
        input_output_aliases={4: 0} if into else {},
        compiler_params=params(10),
        cost_estimate=decode_cost(count * 4 * words * half),
    )(core, token, table, from_hbm(codes), *into)


def matrices_kernel(core_ref, token_ref, *refs, count, by_rows, block):
    tables = refs[:count]
    codes = refs[count : 2 * count]
    weight_ref, token_out_ref, words_ref, came = refs[2 * count :]
    token_out_ref[...] = token_ref[...]
    rows = words_ref.shape[1]
    blocks = words_ref.shape[2] // LANES
    core = core_ref[0]
    first = 0 if by_rows else core * blocks
    row = pl.multiple_of(core * rows, 8) if by_rows else 0

    def far_lanes(at):
        return lanes_at(at) if by_rows else pl.ds(pl.multiple_of((first + at) * LANES, LANES), LANES)

    def fetch(k, at):
        return pltpu.make_async_copy(
            codes[k].at[pl.ds(row, rows), far_lanes(at)], words_ref.at[k, :, lanes_at(at)], came.at[k, at]
        )

    for k in range(count):
        for at in range(blocks):
            fetch(k, at).start()
    for k in range(count):
        for at in range(blocks):
            fetch(k, at).wait()
            decode_lanes(
                words_ref.at[k, :, lanes_at(at)],
                tables[k][0:8, far_lanes(at)],
                tables[k][8:16, far_lanes(at)],
                weight_ref.at[:, lanes_at(k * blocks + at)],
                block,
            )


def decode_matrices(core, token, codes, tables, by_rows):
    count = len(codes)
    words, channels = codes[0].shape
    rows, columns = (words // 2, channels) if by_rows else (words, channels // 2)
    whole = pl.BlockSpec(memory_space=pltpu.VMEM)
    return pl.pallas_call(
        functools.partial(matrices_kernel, count=count, by_rows=by_rows, block=32 if by_rows else 64),
        in_specs=[pl.BlockSpec(memory_space=pltpu.SMEM)]
        + [whole] * (1 + count)
        + [pl.BlockSpec(memory_space=pl.ANY)] * count,
        out_specs=[whole] * 2,
        out_shape=[jax.ShapeDtypeStruct((4 * rows, count * columns), BF)]
        + [jax.ShapeDtypeStruct(token.shape, token.dtype)],
        scratch_shapes=[
            pltpu.VMEM((count, rows, columns), jnp.int32),
            pltpu.SemaphoreType.DMA((count, columns // LANES)),
        ],
        compiler_params=params(10),
        cost_estimate=decode_cost(count * 4 * rows * columns),
    )(core, token, *tables, *[from_hbm(x) for x in codes])


def conv_kernel(
    core_ref, sums_ref, mine_ref, theirs_ref, rim_mine_ref, rim_theirs_ref, gain_ref, shift_ref, bias_ref, time_ref,
    weight_ref, out_ref, act_ref, rim_ref, padded_ref, total_ref, held_ref, arrived, *, members,
):
    slots = held_ref.shape[0]

    def fetch(tap_row):
        slot = tap_row % slots
        return pltpu.make_async_copy(
            weight_ref.at[3 * tap_row : 3 * tap_row + 3], held_ref.at[slot], arrived.at[slot]
        )

    for tap_row in range(slots):
        fetch(tap_row).start()
    channels = gain_ref.shape[-1]
    height, across = mine_ref.shape[:2]
    cells = height * across
    core = core_ref[0]

    parts = rim_theirs_ref[0:16, channels:].astype(F32)
    sums = sums_ref[...] + parts[0:2] + parts[2:4] + parts[4:6]
    sums = jnp.concatenate([sums, jnp.zeros((6, LANES), F32)], axis=0)
    spread = dot(sums, group_matrix(channels, True), precision=lax.Precision.HIGHEST)
    average = spread[0:1] / members
    mean_square = spread[1:2] / members
    scale = lax.rsqrt(mean_square - average * average + 1e-05) * gain_ref[...]
    offset = 0.5 * (shift_ref[...] - average * scale)
    scale = 0.5 * scale
    size = 256
    matrix = shuffle_matrix(64)
    for side, ref in enumerate((mine_ref, theirs_ref)):
        for k in range(0, channels, size):
            lanes = slice(k, k + size)
            value = ref[:, :, lanes].reshape(cells, size).astype(F32)
            value = value * scale[:, lanes] + offset[:, lanes]
            value = value + value * jnp.tanh(value)
            act_ref[side, :, lanes] = dot(value.astype(BF), matrix)
    for side, ref in enumerate((rim_mine_ref, rim_theirs_ref)):
        for k in range(0, channels, size):
            lanes = slice(k, k + size)
            rim_ref[side, :, lanes] = dot(ref[:, lanes], matrix)

    column = iota((across, channels), 0)

    def spread_row(side, line, value, left, right):
        before = jnp.where(column == 0, left, pltpu.roll(value, 1, 0))
        after = jnp.where(column == across - 1, right, pltpu.roll(value, across - 1, 0))
        for at, shifted in enumerate((before, value, after)):
            padded_ref[side, line, :, at * channels : (at + 1) * channels] = shifted.astype(BF)

    for side in range(2):
        other = 1 - side
        is_left = core == side
        for line, base in ((0, 0), (height + 1, 2 * across)):
            corner = across + (height - 1 if line == 0 else 0)
            far = rim_ref[side, base + corner : base + corner + 1]
            next_last = rim_ref[other, base + across - 1 : base + across]
            next_first = rim_ref[other, base : base + 1]
            value = rim_ref[side, base : base + across]
            spread_row(
                side, line, value, jnp.where(is_left, far, next_last), jnp.where(is_left, next_first, far)
            )
        outer_at = 4 * across
        inner_at = 4 * across + height

        @pl.loop(0, height, unroll=height)
        def _(r):
            outer = rim_ref[side, pl.ds(outer_at + r, 1)]
            inner = rim_ref[other, pl.ds(inner_at + r, 1)]
            value = act_ref[side, pl.ds(pl.multiple_of(r * across, across), across)]
            spread_row(
                side, r + 1, value, jnp.where(is_left, outer, inner), jnp.where(is_left, inner, outer)
            )

    half = channels // 2

    def row_product(tap_row):
        fetch(tap_row).wait()
        source = padded_ref[:, tap_row : tap_row + height].reshape(2 * cells, 3 * channels)
        return dot(source, held_ref[tap_row % slots].reshape(3 * channels, half))

    total_ref[...] = row_product(0)
    fetch(2).start()
    total_ref[...] += row_product(1)
    last = row_product(2)
    extra = bias_ref[...] + time_ref[0:1]
    extra = jnp.where(core == 0, extra[:, :half], extra[:, half:])
    for side, ref in enumerate((mine_ref, theirs_ref)):
        image = jnp.where(core == 0, ref[:, :, :half], ref[:, :, half:]).reshape(cells, half).astype(F32)
        rows = slice(side * cells, (side + 1) * cells)
        out_ref[rows] = (image + (total_ref[rows] + last[rows] + extra)).astype(BF)


def convolve(core, sums, mine, theirs, rim_mine, rim_theirs, gain, shift, bias, time_shift, weights, members):
    height, across, channels = mine.shape
    cells = height * across
    half = channels // 2
    whole = pl.BlockSpec(memory_space=pltpu.VMEM)
    small = pl.BlockSpec(memory_space=pltpu.SMEM)
    rim_rows = rim_mine.shape[0]
    return pl.pallas_call(
        functools.partial(conv_kernel, members=members),
        in_specs=[small] + [whole] * 9 + [pl.BlockSpec(memory_space=pl.ANY)],
        out_specs=whole,
        out_shape=jax.ShapeDtypeStruct((2 * cells, half), BF),
        scratch_shapes=[
            pltpu.VMEM((2, cells, channels), F32),
            pltpu.VMEM((2, rim_rows, channels), F32),
            pltpu.VMEM((2, height + 2, across, 3 * channels), BF),
            pltpu.VMEM((2 * cells, half), F32),
            pltpu.VMEM((2, 3, channels, half), BF),
            pltpu.SemaphoreType.DMA((2,)),
        ],
        compiler_params=params(32),
        cost_estimate=pl.CostEstimate(
            flops=36 * cells * channels * half, bytes_accessed=18 * channels * half, transcendentals=2 * cells * channels
        ),
    )(core, sums, mine, theirs, rim_mine, rim_theirs, gain, shift, bias, time_shift, from_hbm(weights))


def stale_kernel(near_ref, far_ref, weight_ref, keys_ref, values_ref):
    pooled = jnp.concatenate([near_ref[...], far_ref[...]], axis=0)
    half = keys_ref.shape[1]
    both = dot(pooled, weight_ref[:, half:]).astype(BF)
    keys_ref[...] = both[:, :half]
    values_ref[...] = both[:, half:]


def stale_pass(near, far, weight):
    rows, channels = near.shape
    half = weight.shape[1] // 3
    whole = pl.BlockSpec(memory_space=pltpu.VMEM)
    return pl.pallas_call(
        stale_kernel,
        in_specs=[whole] * 3,
        out_specs=[whole] * 2,
        out_shape=[jax.ShapeDtypeStruct((2 * rows, half), BF)] * 2,
        compiler_params=params(16),
        cost_estimate=pl.CostEstimate(
            flops=8 * rows * channels * half, bytes_accessed=4 * channels * half, transcendentals=0
        ),
    )(near, far, weight)


def attention_kernel(
    core_ref, mine_ref, theirs_ref, gain_ref, weight_ref, near_keys_ref, near_values_ref,
    beyond_ref, far_ref, out_weight_ref, send_ref, keep_ref, normed_ref, q_ref, k_ref, v_ref, mixed_ref, stale_keys_ref, stale_values_ref,
):
    rows, half = mine_ref.shape
    cells = rows // 2
    channels = 2 * half
    first = core_ref[0] == 0
    matrix = shuffle_matrix(64)
    for side in range(2):
        own = mine_ref[side * cells : (side + 1) * cells].astype(F32)
        other = theirs_ref[(1 - side) * cells : (2 - side) * cells].astype(F32)
        low = jnp.where(first, own, other)
        high = jnp.where(first, other, own)
        residual = jnp.concatenate([low, high], axis=1)
        if side == 0:
            keep_ref[...] = residual
        average = jnp.sum(residual, axis=1, keepdims=True) / channels
        centred = residual - average
        deviation = jnp.sum(centred * centred, axis=1, keepdims=True) / channels
        normed = (centred * lax.rsqrt(deviation + 1e-05) * gain_ref[...]).astype(BF)
        for k in range(0, channels, 256):
            normed_ref[side * cells : (side + 1) * cells, k : k + 256] = dot(
                normed[:, k : k + 256], matrix
            ).astype(BF)
    near_rows = near_keys_ref.shape[0]
    stale_keys_ref[:near_rows] = near_keys_ref[...]
    stale_values_ref[:near_rows] = near_values_ref[...]
    pooled = jnp.concatenate([beyond_ref[...], far_ref[...]], axis=0)
    both = dot(pooled, weight_ref[:, half:]).astype(BF)
    stale_keys_ref[near_rows:] = both[:, :half]
    stale_values_ref[near_rows:] = both[:, half:]
    normed = normed_ref[...]
    projected = dot(normed, weight_ref[...]).astype(BF)
    q_ref[...] = projected[:, :half] * BF(1.0 / math.sqrt(HEAD_DIM))
    k_ref[...] = projected[:, half : 2 * half]
    v_ref[...] = projected[:, 2 * half :]

    ones = jnp.ones((cells, LANES), BF)
    stale_ones = jnp.ones((stale_keys_ref.shape[0], LANES), BF)
    lane = iota((cells, LANES), 1)
    for side in range(2):
        at = slice(side * cells, (side + 1) * cells)
        for pair in range(half // LANES):
            lanes = slice(pair * LANES, (pair + 1) * LANES)
            q = q_ref[at, lanes]
            zero = jnp.zeros_like(q)
            stacked = jnp.concatenate(
                [jnp.where(lane < HEAD_DIM, q, zero), jnp.where(lane < HEAD_DIM, zero, q)], axis=0
            )
            fresh = dot_t(stacked, k_ref[at, lanes])
            stale = dot_t(stacked, stale_keys_ref[:, lanes])
            blocks = [x[:, k : k + LANES] for x in (fresh, stale) for k in range(0, x.shape[1], LANES)]
            highest = jnp.max(functools.reduce(jnp.maximum, blocks), axis=1, keepdims=True)
            fresh = jnp.exp(fresh - highest).astype(BF)
            stale = jnp.exp(stale - highest).astype(BF)
            mixed = dot(fresh, jnp.concatenate([v_ref[at, lanes], ones], axis=1))
            mixed += dot(stale, jnp.concatenate([stale_values_ref[:, lanes], stale_ones], axis=1))
            merged = jnp.where(lane < HEAD_DIM, mixed[:cells, :LANES], mixed[cells:, :LANES])
            weight = jnp.where(lane < HEAD_DIM, mixed[:cells, LANES:], mixed[cells:, LANES:])
            mixed_ref[at, lanes] = (merged / weight).astype(BF)
    mixture = shuffle(mixed_ref[...], 32).astype(BF)
    send_ref[...] = dot(mixture[cells:], out_weight_ref[...]).astype(BF)
    keep_ref[...] += dot(mixture[:cells], out_weight_ref[...])


def attention_pass(core, mine, theirs, gain, projections, near_keys, near_values, beyond, far, out_weight):
    rows, half = mine.shape
    channels = 2 * half
    cells = rows // 2
    whole = pl.BlockSpec(memory_space=pltpu.VMEM)
    small = pl.BlockSpec(memory_space=pltpu.SMEM)
    return pl.pallas_call(
        attention_kernel,
        in_specs=[small] + [whole] * 9,
        out_specs=[whole] * 2,
        out_shape=[
            jax.ShapeDtypeStruct((cells, channels), BF),
            jax.ShapeDtypeStruct((cells, channels), F32),
        ],
        scratch_shapes=[
            pltpu.VMEM((rows, channels), BF),
            pltpu.VMEM((rows, half), BF),
            pltpu.VMEM((rows, half), BF),
            pltpu.VMEM((rows, half), BF),
            pltpu.VMEM((rows, half), BF),
            pltpu.VMEM((4 * far.shape[0], half), BF),
            pltpu.VMEM((4 * far.shape[0], half), BF),
        ],
        compiler_params=params(28),
    )(core, mine, theirs, gain, projections, near_keys, near_values, beyond, far, out_weight)


def swap(values, axis, step):
    count = lax.axis_size(axis)
    return lax.ppermute(values, axis, [(i, i ^ step) for i in range(count)])


def steps_over(axis, first):
    count = lax.axis_size(axis)
    return [(axis, 2 * m - 1) for m in (1 << k for k in range(count.bit_length() - 1)) if m >= first]


def split_sums(sums):
    high = lax.reduce_precision(sums, 8, 7)
    rest = sums - high
    middle = lax.reduce_precision(rest, 8, 7)
    low = rest - middle
    parts = jnp.concatenate([high, middle, low, jnp.zeros((10, LANES), F32)])
    return parts.astype(BF)


def join_sums(parts):
    parts = parts.astype(F32)
    return parts[0:2] + parts[2:4] + parts[4:6]


def tie(first, second):
    return lax.optimization_barrier((first, second))


def on_device(
    image,
    stale_first,
    stale_normed,
    timestep,
    time_weight,
    gain_first,
    shift_first,
    codes_first,
    table_first,
    bias_first,
    attn_gain,
    query_codes,
    query_table,
    key_codes,
    key_table,
    value_codes,
    value_table,
    out_codes,
    out_table,
):
    height, across, channels = image.shape
    cells = height * across
    rows = lax.axis_size("row")
    cols = lax.axis_size("col")
    members = cells * rows * cols * (channels // GROUPS)
    core = (lax.axis_index("col") % 2).astype(jnp.int32)[None]

    sums, edges, pooled, time_shift = first_pass(core, timestep, image, stale_first, stale_normed, time_weight)

    row_at = lax.axis_index("row")
    col_at = lax.axis_index("col")
    beside = jnp.where(core[0] == 0, col_at - 1, col_at + 1)
    hops = steps_over("col", 2) + steps_over("row", 1)
    chunks = [(0, 2), (2, 6), (6, 9)]
    outer = jnp.zeros_like(edges[0])
    above = below = jnp.zeros((height + across, channels), BF)
    near = pooled
    weights = None
    token = sums
    for at, (axis, step) in enumerate(hops):
        last = at == len(hops) - 1
        (sums, near), token = tie((sums, near), token)
        if axis == "col":
            border = edges[0]
        else:
            partner = row_at ^ step
            border = jnp.concatenate([jnp.where(partner > row_at, edges[3], edges[2]), outer])
        parts = jnp.pad(split_sums(sums), ((0, border.shape[0] - across), (0, 0)))
        border = jnp.concatenate([border, parts], axis=1)
        if last:
            got_border = swap(border, axis, step)
            final = (near, axis, step)
            far_near = swap(near, "col", 1)
        else:
            payload = jnp.concatenate([border, jnp.pad(near, ((0, 0), (0, LANES)))])
            got = swap(payload, axis, step)
            got_border = got[: border.shape[0]]
        if at == 1:
            partner_image = swap(image, "col", 1)
        if at < len(chunks):
            weights, token = decode_taps(core, token, codes_first, table_first, weights, *chunks[at])
        elif at == len(chunks):
            projections, token = decode_matrices(
                core, token, (query_codes, key_codes, value_codes), (query_table, key_table, value_table), False
            )
        sums = sums + join_sums(got_border[:across, channels:])
        cells_got = got_border[:, :channels]
        if axis == "col":
            outer = jnp.where((col_at ^ step) == beside, cells_got, outer)
        else:
            above = jnp.where(partner == row_at - 1, cells_got, above)
            below = jnp.where(partner == row_at + 1, cells_got, below)
        if not last:
            near = jnp.concatenate([near, got[border.shape[0] :, :channels]])
    (above, below, sums), token = tie((above, below, sums), token)
    rim = jnp.concatenate([above, below, outer, edges[1]])
    parts = jnp.pad(split_sums(sums), ((0, rim.shape[0] - across), (0, 0)))
    partner_rim = swap(jnp.concatenate([rim, parts], axis=1), "col", 1)
    beyond = swap(*final)
    near_keys, near_values = stale_pass(near, far_near, projections)
    sums, near_keys = tie(sums, near_keys)

    residual = convolve(
        core, sums, image, partner_image, rim, partner_rim, gain_first[None], shift_first[None],
        bias_first[None], time_shift, weights, members,
    )
    (residual, beyond), token = tie((residual, beyond), token)
    partner_residual = swap(residual, "col", 1)
    far = swap(beyond, "col", 1)
    out_weight, _ = decode_matrices(core, token, (out_codes,), (out_table,), True)
    send, keep = attention_pass(
        core, residual, partner_residual, attn_gain[None], projections, near_keys, near_values, beyond, far, out_weight
    )
    output = keep + swap(send, "col", 1).astype(F32)
    return output.astype(BF).reshape(height, across, channels)


def solution(mesh):
    split = P("row", "col", None)
    in_specs = (split,) * 3 + (P(),) * 16
    return jax.shard_map(on_device, mesh=mesh, in_specs=in_specs, out_specs=split, check_vma=False)
```
